512 devices in a mesh: train: 64 (over z_lo, y, core), tensor: 8 (over z_hi, x).
Axes of the slice: x: 4, y: 4, z: 16 (z_hi: 2, z_lo: 8; z = z_hi * 8 + z_lo), core: 2. Of those that a mesh axis runs over, the one named last changes fastest.
Arguments:
- core_left: float32 [32, 65536], P('tensor', 'train'), may hold values from -0.5 to 0.5
- core_right: float32 [16, 196608], P('tensor', 'train'), may hold values from -0.5 to 0.5
- grad_left: float32 [32, 65536], P('tensor', 'train'), may hold values from -6 to 6
- grad_right: float32 [16, 196608], P('tensor', 'train'), may hold values from -6 to 6
- first_left: float32 [32, 65536], P('tensor', 'train'), may hold values from -0.625 to 0.625
- first_right: float32 [16, 196608], P('tensor', 'train'), may hold values from -0.625 to 0.625
- second_left: float32 [32, 65536], P('tensor', 'train'), may hold values from 0.05 to 1
- second_right: float32 [16, 196608], P('tensor', 'train'), may hold values from 0.05 to 1
- up_base: bfloat16 [64, 1536, 4096], P('train', 'tensor'), may hold values from -0.09375 to 0.09375
- down_base: bfloat16 [64, 1536, 4096], P('train', 'tensor'), may hold values from -0.15625 to 0.15625
- states: bfloat16 [4, 512, 4096], P(None, 'train'), may hold values from -6 to 6
- routes: int32 [4, 512, 8], P(None, 'train'), may hold values from 0 to 63, all different within a row; in each aligned block of 8 rows (0 to 7, 8 to 15, ..., all dimensions but the last counted through in order) at most 2 rows name the same one
- gates: float32 [4, 512, 8], P(None, 'train'), may hold values from 0.1 to 0.4
Outputs:
- mixed: bfloat16 [4, 512, 4096], P(None, 'train', 'tensor')
- left_next: float32 [32, 65536], P('tensor', 'train')
- right_next: float32 [16, 196608], P('tensor', 'train')
- first_left_next: float32 [32, 65536], P('tensor', 'train')
- first_right_next: float32 [16, 196608], P('tensor', 'train')
- second_left_next: float32 [32, 65536], P('tensor', 'train')
- second_right_next: float32 [16, 196608], P('tensor', 'train')
The draws below stay inside these ranges and needn't reach their ends.
Inputs may be any that keep to these rules, and one draw needn't show every extreme that they name: `routes`: each row names 8 different experts; among the 8 rows n with n // 8 equal, for one step, no expert is named more than 2 times.
All inputs are finite; a program needn't handle non-finite values.
Results may differ from the reference program's by a relative error of at most 0.019.
Values may be sent and summed in bfloat16 or wider, within the bound.
A program may use at most 64 MiB of HBM per device.

```python
import math
import jax
import jax.numpy as jnp
import numpy as np
from jax import lax

D = 4096
FF = 1536
TOP = 8
I1 = 64
J1 = 32
RANK = 16
STEPS = 4
ROWS_DEV = 8
I2 = 64
J2 = 48
EXPERTS = 64
ROWS = 512
CAP = 2
N_TRAIN = 64
N_TENSOR = 8


def level_of(key, shape, shards, least, largest):
    gain, own = 1.0, jax.random.fold_in(key, 6)
    for axis_at, shards_of in shards:
        steps = jnp.exp(jax.random.uniform(jax.random.fold_in(own, axis_at), (shards_of,), jnp.float32, least / len(shards), largest / len(shards)))
        gain = gain * jnp.repeat(steps, shape[axis_at] // shards_of).reshape([-1 if axis == axis_at else 1 for axis in range(len(shape))])
    return gain


def deal_out(stream_key, own, number, rows, number_of, top, most, lean):
    sequence = jax.random.permutation(stream_key, number_of)
    packed, ordinary = shares(number_of, rows * top, most, lean, True), shares(number_of, rows * top, most, lean, False)
    places = jnp.arange(number_of)

    def named(sizes, rotation):
        used = int((sizes > 0).sum())
        fixed = max(1, used // 4)
        moved = fixed + (places - fixed + rotation * (used - fixed)) % max(1, number_of - fixed)
        return jnp.zeros((number_of,), jnp.int32).at[sequence[jnp.where(places < fixed, places, moved)]].set(jnp.asarray(sizes, jnp.int32))

    sizes = jnp.where(number % 4 == 0, named(packed, number // 4), named(ordinary, number - number // 4 - 1))
    mixed = jax.random.permutation(jax.random.fold_in(own, 3), number_of)
    source_of, sink = mixed[0:number_of // 2 * 2:2], mixed[1:number_of // 2 * 2:2]
    slack = jnp.minimum(sizes[source_of] - 1, most - sizes[sink]) // 2
    slack = jnp.where((source_of == sequence[0]) | (sink == sequence[0]) | (sizes[sink] == 0), 0, jnp.maximum(slack, 0))
    moved = jax.random.randint(jax.random.fold_in(own, 4), (number_of // 2,), 0, 1 << 20) % (slack + 1)
    sizes = sizes.at[source_of].add(-moved).at[sink].add(moved)
    items = jnp.searchsorted(jnp.cumsum(sizes), jnp.arange(rows * top), side="right").astype(jnp.int32)
    table = items.reshape(top, rows).T
    table = table[jax.random.permutation(jax.random.fold_in(own, 1), rows)]
    rotation = jax.random.randint(jax.random.fold_in(own, 2), (rows, 1), 0, top)
    return jnp.take_along_axis(table, (jnp.arange(top)[None, :] + rotation) % top, axis=1)


def shares(amount, total, reach, slope, full):
    weights = [(1 << 20) // math.isqrt(rank ** slope) + 1 for rank in range(1, amount + 1)]
    largest = reach if full else min(reach, max(-(-total // amount), total * weights[0] // sum(weights)))
    least = 1 if total - largest >= amount - 1 else 0
    counts, surplus = [largest] + [least] * (amount - 1), total - largest - least * (amount - 1)
    while surplus > 0:
        movable = [i for i in range(1, amount) if counts[i] < largest] or [i for i in range(1, amount) if counts[i] < reach]
        whole, remaining = sum([weights[i] for i in movable]), surplus
        for i in movable:
            extra = min(reach - counts[i], max(1, remaining * weights[i] // whole), surplus)
            counts[i] = counts[i] + extra
            surplus = surplus - extra
    return np.array(counts)


def centred(rng, shape, scale, reach, split=(), held_as=jnp.bfloat16):
    entries = jax.random.normal(rng, shape, jnp.float32) * scale
    if len(split) > 0:
        entries = level_of(rng, shape, split, -0.22, 0.18) * entries
    return jnp.clip(entries, min=-reach, max=reach).astype(held_as)


def setup_inputs(seed: int = 0) -> dict:
    arg_keys = jax.random.split(jax.random.key(seed), 14)
    core_left = centred(arg_keys[0], (J1, I1 * RANK * EXPERTS), 0.08, 0.5, ((0, 8), (1, 64)), jnp.float32)
    core_right = centred(arg_keys[1], (RANK, J2 * I2 * EXPERTS), 0.08, 0.5, ((0, 8), (1, 64)), jnp.float32)
    grad_left = centred(arg_keys[2], (J1, I1 * RANK * EXPERTS), 1.0, 6.0, ((0, 8), (1, 64)), jnp.float32)
    grad_right = centred(arg_keys[3], (RANK, J2 * I2 * EXPERTS), 1.0, 6.0, ((0, 8), (1, 64)), jnp.float32)
    first_left = centred(arg_keys[4], (J1, I1 * RANK * EXPERTS), 0.1, 0.625, ((0, 8), (1, 64)), jnp.float32)
    first_right = centred(arg_keys[5], (RANK, J2 * I2 * EXPERTS), 0.1, 0.625, ((0, 8), (1, 64)), jnp.float32)
    second_left = jnp.clip(jnp.exp(math.log(1.0) - 2.9957323 * jax.random.uniform(arg_keys[6], (J1, I1 * RANK * EXPERTS), jnp.float32) ** level_of(arg_keys[6], (J1, I1 * RANK * EXPERTS), ((0, 8), (1, 64)), -0.2, 0.2)), 0.05, 1.0)
    second_right = jnp.clip(jnp.exp(math.log(1.0) - 2.9957323 * jax.random.uniform(arg_keys[7], (RANK, J2 * I2 * EXPERTS), jnp.float32) ** level_of(arg_keys[7], (RANK, J2 * I2 * EXPERTS), ((0, 8), (1, 64)), -0.2, 0.2)), 0.05, 1.0)
    up_base = centred(arg_keys[8], (EXPERTS, FF, D), D ** -0.5, 0.09375, ((0, 64), (1, 8)))
    down_base = centred(arg_keys[9], (EXPERTS, FF, D), FF ** -0.5, 0.15625, ((0, 64), (1, 8)))
    states = centred(arg_keys[10], (STEPS, ROWS, D), 1.0, 6.0, ((1, 64),))
    routes_keys = jax.random.split(jax.random.fold_in(arg_keys[11], 1), STEPS * ROWS // ROWS_DEV)
    routes_turns = jax.random.permutation(jax.random.fold_in(arg_keys[11], 3), STEPS * ROWS // ROWS_DEV)
    routes = jax.vmap(lambda own, number: deal_out(jax.random.fold_in(arg_keys[11], 2), own, number, ROWS_DEV, EXPERTS, TOP, CAP, 2))(routes_keys, routes_turns).reshape((STEPS, ROWS, TOP))
    gates = jnp.clip(0.1 + 0.3 * jax.random.uniform(arg_keys[12], (STEPS, ROWS, TOP), jnp.float32) ** level_of(arg_keys[12], (STEPS, ROWS, TOP), ((1, 64),), -0.2, 0.2), 0.1, 0.4)
    return dict(core_left=core_left, core_right=core_right, grad_left=grad_left, grad_right=grad_right, first_left=first_left, first_right=first_right, second_left=second_left, second_right=second_right, up_base=up_base, down_base=down_base, states=states, routes=routes, gates=gates)


BETA_ONE = 0.9
BETA_TWO = 0.999
LEARN_RATE = 0.01
WEIGHT_DECAY = 0.1
EPSILON = 1e-08
STEP_NUMBER = 10.0

def adamw_update(value_now, gradient, first_moment, second_moment):
    first_next = BETA_ONE * first_moment + (1.0 - BETA_ONE) * gradient
    second_next = BETA_TWO * second_moment + (1.0 - BETA_TWO) * gradient * gradient
    first_scale = 1.0 - BETA_ONE ** STEP_NUMBER
    second_scale = 1.0 - BETA_TWO ** STEP_NUMBER
    update = first_next / first_scale / (jnp.sqrt(second_next / second_scale) + EPSILON)
    value_next = value_now - LEARN_RATE * (update + WEIGHT_DECAY * value_now)
    return (value_next, first_next, second_next)

def expert_output(pieces):
    rows_in, up_weight, down_weight, left_core, right_core = pieces
    delta = jnp.einsum('jar,rkb->jkab', left_core.astype(jnp.float32), right_core.astype(jnp.float32), precision=lax.Precision.HIGHEST).reshape(FF, D)
    up_eff = (up_weight.astype(jnp.float32) + delta).astype(jnp.bfloat16)
    hidden = jax.nn.silu(jnp.dot(rows_in, up_eff.T, preferred_element_type=jnp.float32)).astype(jnp.bfloat16)
    grouped = hidden.reshape(rows_in.shape[0], N_TENSOR, FF // N_TENSOR).astype(jnp.float32)
    down_grouped = down_weight.reshape(N_TENSOR, FF // N_TENSOR, D).astype(jnp.float32)
    parts = jnp.einsum('mpf,pfd->pmd', grouped, down_grouped, precision=lax.Precision.HIGHEST).astype(jnp.bfloat16)
    return lax.optimization_barrier(jnp.sum(parts.astype(jnp.float32), axis=0))

def reference(core_left, core_right, grad_left, grad_right, first_left, first_right, second_left, second_right, up_base, down_base, states, routes, gates):
    left_next, first_left_next, second_left_next = adamw_update(core_left, grad_left, first_left, second_left)
    right_next, first_right_next, second_right_next = adamw_update(core_right, grad_right, first_right, second_right)
    left_table = left_next.astype(jnp.bfloat16).reshape(J1, I1, RANK, EXPERTS).transpose(3, 0, 1, 2)
    right_table = right_next.astype(jnp.bfloat16).reshape(RANK, J2, I2, EXPERTS).transpose(3, 0, 1, 2)
    slots_total = N_TRAIN * CAP
    onehot = (routes[..., None] == jnp.arange(EXPERTS, dtype=jnp.int32)).astype(jnp.int32)
    blocked = onehot.reshape(STEPS, N_TRAIN, ROWS_DEV * TOP, EXPERTS)
    before = jnp.cumsum(blocked, axis=2) - blocked
    slot_index = lax.optimization_barrier(jnp.sum(before * blocked, axis=3)).reshape(STEPS, ROWS, TOP)
    block_index = jnp.arange(ROWS, dtype=jnp.int32) // ROWS_DEV
    position = block_index[None, :, None] * CAP + slot_index
    step_index = jnp.arange(STEPS, dtype=jnp.int32)[:, None, None]
    flat_index = ((routes * STEPS + step_index) * slots_total + position).astype(jnp.int32).reshape(-1)
    spread = jnp.broadcast_to(states[:, :, None, :], (STEPS, ROWS, TOP, D)).reshape(-1, D)
    buffer = jnp.zeros((EXPERTS * STEPS * slots_total, D), jnp.bfloat16).at[flat_index].set(spread)
    buffer = buffer.reshape(EXPERTS, STEPS * slots_total, D)
    results = lax.map(expert_output, (buffer, up_base, down_base, left_table, right_table))
    looked = results.reshape(EXPERTS * STEPS * slots_total, D)[flat_index].reshape(STEPS, ROWS, TOP, D)
    mixed = lax.optimization_barrier(jnp.sum(gates[..., None] * looked, axis=2)).astype(jnp.bfloat16)
    return (mixed, left_next, right_next, first_left_next, first_right_next, second_left_next, second_right_next)
```

```python
import jax
import jax.numpy as jnp
from jax import lax
from jax.experimental import pallas as pl
from jax.experimental.pallas import tpu as pltpu
from jax.sharding import PartitionSpec as P

MESH = pl.DeviceIdType.MESH
BF16 = jnp.bfloat16
F32 = jnp.float32

BETA_ONE = 0.9
BETA_TWO = 0.999
LEARN_RATE = 0.01
WEIGHT_DECAY = 0.1
EPSILON = 1e-08
STEP_NUMBER = 10.0

VMEM_LIMIT = 48 * 1024 * 1024


def adamw_update(value_now, gradient, first_moment, second_moment):
    first_next = BETA_ONE * first_moment + (1.0 - BETA_ONE) * gradient
    second_next = BETA_TWO * second_moment + (1.0 - BETA_TWO) * gradient * gradient
    first_scale = 1.0 - BETA_ONE**STEP_NUMBER
    second_scale = 1.0 - BETA_TWO**STEP_NUMBER
    update = first_next / first_scale / (jnp.sqrt(second_next / second_scale) + EPSILON)
    value_next = value_now - LEARN_RATE * (update + WEIGHT_DECAY * value_now)
    return (value_next, first_next, second_next)


class Place:
    def __init__(self):
        self.train = lax.axis_index("train")
        self.tensor = lax.axis_index("tensor")
        self.core = self.train % 2
        self.y = (self.train // 2) % 4
        self.z_lo = self.train // 8
        self.x = self.tensor % 4
        self.z_hi = self.tensor // 4
        self.z = self.z_hi * 8 + self.z_lo

    def at_z(self, z):
        z = (z + 16) % 16
        return ((z % 8) * 8 + self.y * 2 + self.core, (z // 8) * 4 + self.x)

    def at_y(self, y):
        return (self.z_lo * 8 + ((y + 4) % 4) * 2 + self.core, self.tensor)

    def at_x(self, x):
        return (self.train, self.z_hi * 4 + (x + 4) % 4)

    def twin(self):
        return (self.train + 1 - 2 * self.core, self.tensor)

    def other_half(self):
        return (self.train, (1 - self.z_hi) * 4 + self.x)


def push(src, dst, sems, index, device):
    copy = pltpu.make_async_remote_copy(
        src_ref=src,
        dst_ref=dst,
        send_sem=sems.at[0, index],
        recv_sem=sems.at[1, index],
        device_id=device,
        device_id_type=MESH,
    )
    copy.start()
    return copy


def signal(device):
    pl.semaphore_signal(
        pltpu.get_barrier_semaphore(), inc=1, device_id=device, device_id_type=MESH
    )


def gather_kernel(
    up, down, rows, message,
    up_all, down_all, rows_all, message_all, relay,
    local_sem, z_sem, y_sem, far_sem, twin_sem, weight_sem, relay_sem, small_sem, spread_sem,
):
    at = Place()
    train, tensor, x, y, z_lo, core = at.train, at.tensor, at.x, at.y, at.z_lo, at.core

    @pl.loop(1, 64)
    def _(step):
        signal(((train + step) % 64, tensor))

    for device in (at.at_z(at.z + 1), at.at_z(at.z - 1), at.other_half()):
        signal(device)
    for step in (1, 2, 3):
        signal(at.at_x(x + step))
    pl.semaphore_wait(pltpu.get_barrier_semaphore(), 69)

    weights = ((up, up_all), (down, down_all))
    own = []
    for w, (src, dst) in enumerate(weights):
        for half in (0, 1):
            columns = pl.ds(pl.multiple_of((half * 4 + x) * 512, 512), 512)
            own.append((src.at[:, columns], dst.at[half, x]))
    own.append((rows, rows_all.at[z_lo, y, core]))
    own.append((message.at[train], message_all.at[tensor, train]))
    own = [pltpu.make_async_copy(s, d, local_sem.at[i]) for i, (s, d) in enumerate(own)]
    for copy in own:
        copy.start()

    sent = []
    first = rows_all.at[z_lo, y, core]
    z_right = [push(rows, first, z_sem, 0, at.at_z(at.z + 1))]
    z_left = [push(rows, first, z_sem, 4, at.at_z(at.z - 1))]
    y_right = [push(rows, first, y_sem, 0, at.at_y(y + 1))]
    y_left = [push(rows, first, y_sem, 8, at.at_y(y - 1))]

    def small(step):
        target = (train + step) % 64
        return pltpu.make_async_remote_copy(
            src_ref=message.at[target],
            dst_ref=message_all.at[tensor, train],
            send_sem=small_sem.at[0],
            recv_sem=small_sem.at[1],
            device_id=(target, tensor),
            device_id_type=MESH,
        )

    @pl.loop(1, 64)
    def _(step):
        small(step).start()

    direct, onward = [], {}
    for w, (src, dst) in enumerate(weights):
        for way, step in ((0, 1), (1, -1)):
            far = (x + 2) % 4
            columns = pl.ds(pl.multiple_of((way * 4 + far) * 512, 512), 512)
            direct.append(
                push(src.at[:, columns], relay.at[w, way], relay_sem, w * 2 + way, at.at_x(x + step))
            )
            near = (x + step + 4) % 4
            for half in (0, 1):
                columns = pl.ds(pl.multiple_of((half * 4 + near) * 512, 512), 512)
                sent.append(
                    push(
                        src.at[:, columns], dst.at[half, x],
                        weight_sem, w * 4 + way * 2 + half, at.at_x(near),
                    )
                )

    def pass_on(w):
        dst = weights[w][1]
        for way, step in ((0, 1), (1, -1)):
            direct[w * 2 + way].wait_recv()
            source = (x - step + 4) % 4
            onward[w, way] = push(
                relay.at[w, way], dst.at[way, source],
                relay_sem, 4 + w * 2 + way, at.at_x(x + step),
            )

    blocks = [z_lo]
    for order in range(1, 8):
        step = (order + 1) // 2
        if order % 2 == 1:
            z_right[step - 1].wait_recv()
            block = (z_lo - step + 8) % 8
            if step < 4:
                here = rows_all.at[block, y, core]
                z_right.append(push(here, here, z_sem, step, at.at_z(at.z + 1)))
        else:
            z_left[step - 1].wait_recv()
            block = (z_lo + step) % 8
            if step < 3:
                here = rows_all.at[block, y, core]
                z_left.append(push(here, here, z_sem, 4 + step, at.at_z(at.z - 1)))
        blocks.append(block)
        here = rows_all.at[block, y, core]
        y_right.append(push(here, here, y_sem, order, at.at_y(y + 1)))
        y_left.append(push(here, here, y_sem, 8 + order, at.at_y(y - 1)))

    all_but_one = pltpu.make_async_remote_copy(
        src_ref=message.at[pl.ds(0, 63)],
        dst_ref=message_all.at[tensor, pl.ds(0, 63)],
        send_sem=small_sem.at[0],
        recv_sem=small_sem.at[1],
        device_id=(train, tensor),
        device_id_type=MESH,
    )
    all_but_one.wait_recv()
    own[5].wait()
    here = message_all.at[tensor]
    across = push(here, here, spread_sem, 0, at.other_half())
    spread = [push(here, here, spread_sem, step, at.at_x(x + step)) for step in (1, 2, 3)]

    far_copies = []
    for order, block in enumerate(blocks):
        y_right[order].wait_recv()
        y_left[order].wait_recv()
        if order % 2 == 0:
            here = rows_all.at[block, (y + 3) % 4, core]
            far_copies.append(push(here, here, far_sem, order, at.at_y(y + 1)))
        else:
            here = rows_all.at[block, (y + 1) % 4, core]
            far_copies.append(push(here, here, far_sem, order, at.at_y(y - 1)))

    pass_on(0)

    across.wait_recv()
    here = message_all.at[(1 - at.z_hi) * 4 + x]
    for step in (1, 2, 3):
        spread.append(push(here, here, spread_sem, 3 + step, at.at_x(x + step)))

    own[4].wait()
    twin_copies = []
    for order, block in enumerate(blocks):
        far_copies[order].wait_recv()
        here = rows_all.at[block, :, core]
        twin_copies.append(push(here, here, twin_sem, order, at.twin()))

    pass_on(1)

    for copy in spread + sent + list(onward.values()) + twin_copies:
        copy.wait_recv()
    for copy in own[:4]:
        copy.wait()
    for copy in (
        z_right + z_left + y_right + y_left + far_copies + twin_copies
        + [across] + spread + sent + direct + list(onward.values()) + [all_but_one]
    ):
        copy.wait_send()


def dma_sems(count):
    return pltpu.SemaphoreType.DMA((2, count))


def gather_all(up, down, rows, message):
    return pl.pallas_call(
        gather_kernel,
        out_shape=(
            jax.ShapeDtypeStruct((2, 4, 192, 512), BF16),
            jax.ShapeDtypeStruct((2, 4, 192, 512), BF16),
            jax.ShapeDtypeStruct((8, 4, 2, 32, 1024), BF16),
            jax.ShapeDtypeStruct((8, 64, 2, 128), F32),
            jax.ShapeDtypeStruct((2, 2, 192, 512), BF16),
        ),
        in_specs=[pl.BlockSpec(memory_space=pl.ANY)] * 4,
        out_specs=[pl.BlockSpec(memory_space=pl.ANY)] * 5,
        scratch_shapes=[
            pltpu.SemaphoreType.DMA((6,)),
            dma_sems(7),
            dma_sems(16),
            dma_sems(8),
            dma_sems(8),
            dma_sems(8),
            dma_sems(8),
            pltpu.SemaphoreType.DMA((2,)),
            dma_sems(7),
        ],
        compiler_params=pltpu.CompilerParams(collective_id=0, has_side_effects=True),
        name="gather_all",
    )(up, down, rows, message)


def up_kernel(up_ref, left_ref, right_ref, rows_ref, out_ref, weight, total):
    half = pl.program_id(1)
    for j in range(4):
        for lane in range(4):
            lanes = slice(lane * 128, lane * 128 + 128)
            delta = jnp.zeros((48, 128), F32)
            for r in range(16):
                delta = delta + right_ref[r] * left_ref[j, r : r + 1, lanes]
            units = slice(j * 48, j * 48 + 48)
            weight[units, lanes] = (up_ref[units, lanes].astype(F32) + delta).astype(BF16)
    term = lax.dot_general(
        weight[...], rows_ref[...], (((1,), (1,)), ((), ())), preferred_element_type=F32
    )

    @pl.when(half == 0)
    def _():
        total[...] = term

    @pl.when(half == 1)
    def _():
        out_ref[...] = (total[...] + term).astype(BF16)


def up_project(up_all, left, right, rows):
    return pl.pallas_call(
        up_kernel,
        grid=(4, 2),
        out_shape=jax.ShapeDtypeStruct((4, 192, 512), BF16),
        in_specs=[
            pl.BlockSpec((None, None, 192, 512), lambda g, h: (h, g, 0, 0)),
            pl.BlockSpec((None, None, 4, 16, 512), lambda g, h: (h, g, 0, 0, 0)),
            pl.BlockSpec((16, 48, 128), lambda g, h: (0, 0, 0)),
            pl.BlockSpec((512, 512), lambda g, h: (0, h)),
        ],
        out_specs=pl.BlockSpec((None, 192, 512), lambda g, h: (g, 0, 0)),
        scratch_shapes=[pltpu.VMEM((192, 512), BF16), pltpu.VMEM((192, 512), F32)],
        compiler_params=pltpu.CompilerParams(vmem_limit_bytes=VMEM_LIMIT),
        name="up_project",
    )(up_all, left, right, rows)


def hidden_kernel(part, out, far, near, passed, hidden, far_sem, near_sem, out_sem):
    at = Place()
    x = at.x
    right, left = at.at_x(x + 1), at.at_x(x - 1)
    signal(right)
    signal(left)
    pl.semaphore_wait(pltpu.get_barrier_semaphore(), 2)

    right_x, left_x, far_x = (x + 1) % 4, (x + 3) % 4, (x + 2) % 4
    top, low = pl.ds(0, 96), pl.ds(96, 96)
    copies = [
        push(part.at[far_x, top], far.at[0], far_sem, 0, right),
        push(part.at[far_x, low], far.at[1], far_sem, 1, left),
        push(part.at[right_x, low], near.at[0, low], near_sem, 0, right),
        push(part.at[left_x, top], near.at[1, top], near_sem, 1, left),
    ]
    copies[0].wait_recv()
    passed[0] = (part[right_x, top].astype(F32) + far[0].astype(F32)).astype(BF16)
    copies.append(push(passed.at[0], near.at[0, top], near_sem, 2, right))
    copies[1].wait_recv()
    passed[1] = (part[left_x, low].astype(F32) + far[1].astype(F32)).astype(BF16)
    copies.append(push(passed.at[1], near.at[1, low], near_sem, 3, left))
    for copy in copies[2:]:
        copy.wait_recv()

    value = part[x].astype(F32) + near[0].astype(F32) + near[1].astype(F32)
    hidden[x] = (value / (1.0 + jnp.exp(-value))).astype(BF16)
    here = hidden.at[x]
    from_left = push(here, here, out_sem, 0, right)
    from_right = push(here, here, out_sem, 1, left)
    from_left.wait_recv()
    here = hidden.at[left_x, top]
    far_top = push(here, here, out_sem, 2, right)
    from_right.wait_recv()
    here = hidden.at[right_x, low]
    far_low = push(here, here, out_sem, 3, left)
    far_top.wait_recv()
    far_low.wait_recv()
    for copy in copies + [from_left, from_right, far_top, far_low]:
        copy.wait_send()
    out[...] = hidden[...]


def hidden_sum(part):
    return pl.pallas_call(
        hidden_kernel,
        out_shape=jax.ShapeDtypeStruct((4, 192, 512), BF16),
        in_specs=[pl.BlockSpec(memory_space=pltpu.VMEM)],
        out_specs=pl.BlockSpec(memory_space=pltpu.VMEM),
        scratch_shapes=[
            pltpu.VMEM((2, 96, 512), BF16),
            pltpu.VMEM((2, 192, 512), BF16),
            pltpu.VMEM((2, 96, 512), BF16),
            pltpu.VMEM((4, 192, 512), BF16),
            dma_sems(2),
            dma_sems(4),
            dma_sems(4),
        ],
        compiler_params=pltpu.CompilerParams(
            collective_id=1, has_side_effects=True, vmem_limit_bytes=VMEM_LIMIT
        ),
        name="hidden_sum",
    )(part)


def down_kernel(hidden_ref, down_ref, combine_ref, out_ref):
    part = lax.dot_general(
        hidden_ref[...], down_ref[...], (((0,), (0,)), ((), ())), preferred_element_type=F32
    ).astype(BF16)
    for group in range(8):
        mixed = jnp.dot(
            combine_ref[group], part[group * 64 : group * 64 + 64], preferred_element_type=F32
        ).astype(BF16)
        for y in range(4):
            for core in range(2):
                at = (y * 2 + core) * 32
                out_ref[core, y, group] = mixed[at : at + 32]


def down_project(hidden, down_all, combine):
    return pl.pallas_call(
        down_kernel,
        grid=(2,),
        out_shape=jax.ShapeDtypeStruct((2, 4, 16, 32, 512), BF16),
        in_specs=[
            pl.BlockSpec((768, 512), lambda h: (0, 0)),
            pl.BlockSpec((None, 768, 512), lambda h: (h, 0, 0)),
            pl.BlockSpec((8, 256, 64), lambda h: (0, 0, 0)),
        ],
        out_specs=pl.BlockSpec((2, 4, 8, 32, 512), lambda h: (0, 0, h, 0, 0)),
        compiler_params=pltpu.CompilerParams(vmem_limit_bytes=VMEM_LIMIT),
        name="down_project",
    )(hidden, down_all, combine)


def add_pairs(dst, count, *terms):
    @pl.loop(0, count)
    def _(i):
        total = terms[0](i).astype(F32)
        for term in terms[1:]:
            total = total + term(i).astype(F32)
        dst[i] = total.astype(BF16)


def mix_kernel(
    part, out, twin_in, sums, far, near, line, right_in, left_in, right_out, left_out,
    twin_sem, far_sem, near_sem, right_sem, left_sem,
):
    at = Place()
    y, z, core = at.y, at.z, at.core
    y_right, y_left = at.at_y(y + 1), at.at_y(y - 1)
    z_right, z_left = at.at_z(z + 1), at.at_z(z - 1)
    for device in (at.twin(), y_right, y_left, z_right, z_left):
        signal(device)
    pl.semaphore_wait(pltpu.get_barrier_semaphore(), 5)

    order = [(y + 2) % 4, (y + 1) % 4, (y + 3) % 4, y]
    twins = [
        push(part.at[1 - core, to], twin_in.at[to], twin_sem, i, at.twin())
        for i, to in enumerate(order)
    ]

    def sum_cores(i):
        to = order[i]
        twins[i].wait_recv()
        add_pairs(sums.at[i], 16, lambda k: part[core, to, k], lambda k: twin_in[to, k])

    top, low = pl.ds(0, 8), pl.ds(8, 8)
    sum_cores(0)
    copies = [
        push(sums.at[0, top], far.at[0], far_sem, 0, y_right),
        push(sums.at[0, low], far.at[1], far_sem, 1, y_left),
    ]
    sum_cores(1)
    copies.append(push(sums.at[1, low], near.at[0, low], near_sem, 0, y_right))
    sum_cores(2)
    copies.append(push(sums.at[2, top], near.at[1, top], near_sem, 1, y_left))
    copies[0].wait_recv()
    add_pairs(sums.at[1], 8, lambda k: sums[1, k], lambda k: far[0, k])
    copies.append(push(sums.at[1, top], near.at[0, top], near_sem, 2, y_right))
    copies[1].wait_recv()
    add_pairs(sums.at[2, low], 8, lambda k: sums[2, 8 + k], lambda k: far[1, k])
    copies.append(push(sums.at[2, low], near.at[1, low], near_sem, 3, y_left))
    sum_cores(3)
    for copy in copies[2:]:
        copy.wait_recv()
    add_pairs(line, 16, lambda k: sums[3, k], lambda k: near[0, k], lambda k: near[1, k])

    rights, lefts = [], []
    for step in range(8):
        value = line[(z + 8 - step) % 16].astype(F32)
        if step > 0:
            rights[step - 1].wait_recv()
            value = value + right_in[step - 1].astype(F32)
        right_out[step] = value.astype(BF16)
        rights.append(push(right_out.at[step], right_in.at[step], right_sem, step, z_right))
        if step < 7:
            value = line[(z + 9 + step) % 16].astype(F32)
            if step > 0:
                lefts[step - 1].wait_recv()
                value = value + left_in[step - 1].astype(F32)
            left_out[step] = value.astype(BF16)
            lefts.append(push(left_out.at[step], left_in.at[step], left_sem, step, z_left))
    lefts[6].wait_recv()
    rights[7].wait_recv()
    value = line[z].astype(F32) + right_in[7].astype(F32) + left_in[6].astype(F32)
    out[...] = value.astype(BF16)
    for copy in twins + copies + rights + lefts:
        copy.wait_send()


def mix_sum(part):
    return pl.pallas_call(
        mix_kernel,
        out_shape=jax.ShapeDtypeStruct((32, 512), BF16),
        in_specs=[pl.BlockSpec(memory_space=pltpu.VMEM)],
        out_specs=pl.BlockSpec(memory_space=pltpu.VMEM),
        scratch_shapes=[
            pltpu.VMEM((4, 16, 32, 512), BF16),
            pltpu.VMEM((4, 16, 32, 512), BF16),
            pltpu.VMEM((2, 8, 32, 512), BF16),
            pltpu.VMEM((2, 16, 32, 512), BF16),
            pltpu.VMEM((16, 32, 512), BF16),
            pltpu.VMEM((8, 32, 512), BF16),
            pltpu.VMEM((7, 32, 512), BF16),
            pltpu.VMEM((8, 32, 512), BF16),
            pltpu.VMEM((7, 32, 512), BF16),
            dma_sems(4),
            dma_sems(2),
            dma_sems(4),
            dma_sems(8),
            dma_sems(7),
        ],
        compiler_params=pltpu.CompilerParams(
            collective_id=2, has_side_effects=True, vmem_limit_bytes=VMEM_LIMIT
        ),
        name="mix_sum",
    )(part)


def body(
    core_left,
    core_right,
    grad_left,
    grad_right,
    first_left,
    first_right,
    second_left,
    second_right,
    up_base,
    down_base,
    states,
    routes,
    gates,
):
    left_next, first_left_next, second_left_next = adamw_update(
        core_left, grad_left, first_left, second_left
    )
    right_next, first_right_next, second_right_next = adamw_update(
        core_right, grad_right, first_right, second_right
    )
    tensor = lax.axis_index("tensor")
    x, z_hi = tensor % 4, tensor // 4

    chosen = (routes[..., None] == jnp.arange(64, dtype=jnp.int32)).astype(F32)
    taken = jnp.sum(chosen, axis=2)
    weight = jnp.sum(chosen * gates[..., None], axis=2)
    earlier = jnp.cumsum(taken, axis=1) - taken
    slot = taken * (earlier + 1.0)
    message = jnp.concatenate(
        [
            lax.reduce_precision(left_next, 8, 7).reshape(64, 64),
            lax.reduce_precision(right_next, 8, 7).reshape(96, 64),
            slot.reshape(32, 64),
            weight.reshape(32, 64),
            jnp.zeros((32, 64), F32),
        ],
        axis=0,
    )
    message = message.T.reshape(64, 2, 128)
    rows = lax.dynamic_index_in_dim(states.reshape(32, 2, 4, 512), x, 2, keepdims=False)
    up_all, down_all, rows_all, message_all, _ = gather_all(
        up_base[0], down_base[0], rows.reshape(32, 1024), message
    )

    message_all = message_all.reshape(8, 64, 256)
    left = lax.dynamic_slice_in_dim(message_all[:, :, :64], z_hi * 4, 4, 0)
    left = left.reshape(4, 2, 4, 8, 4, 16)
    left = lax.dynamic_index_in_dim(left, x, 2, keepdims=False)
    left = left.transpose(1, 0, 3, 4, 2).reshape(512, 8).astype(BF16)
    spread = (jnp.arange(8)[:, None] == jnp.arange(512)[None, :] // 64).astype(BF16)
    left = jnp.dot(left, spread, preferred_element_type=F32).reshape(2, 4, 4, 16, 512)
    right = message_all[:, :, 64:160].reshape(8, 64, 2, 48)
    right = right.transpose(0, 2, 1, 3).reshape(16, 48, 64)
    right = jnp.concatenate([right, right], axis=2)

    own = lax.dynamic_index_in_dim(message_all, tensor, 0, keepdims=False)
    slot = own[:, 160:192].reshape(8, 256)
    weight = own[:, 192:224].reshape(8, 256)
    slots, places = jnp.arange(64), jnp.arange(256)
    match = (slots[:, None] // 2 == places[None, :] // 8)[None] & (
        slot[:, None, :] == (slots % 2 + 1).astype(F32)[None, :, None]
    )
    picked = jnp.einsum(
        "gsr,grd->gsd",
        match.astype(BF16),
        rows_all.reshape(8, 256, 1024),
        preferred_element_type=F32,
    ).astype(BF16)
    match = (slots[None, :] // 2 == places[:, None] // 8)[None] & (
        slot[:, :, None] == (slots % 2 + 1).astype(F32)[None, None, :]
    )
    combine = jnp.where(match, weight[:, :, None], 0.0).astype(BF16)

    part = up_project(up_all, left, right, picked.reshape(512, 1024))
    hidden = hidden_sum(part)
    part = down_project(hidden.reshape(768, 512), down_all.reshape(2, 768, 512), combine)
    mixed = mix_sum(part).reshape(4, 8, 512)
    return (
        mixed,
        left_next,
        right_next,
        first_left_next,
        first_right_next,
        second_left_next,
        second_right_next,
    )


def solution(mesh):
    cores = (P("tensor", "train"),) * 6
    in_specs = cores + (P("tensor", "train"),) * 2 + (
        P("train", "tensor", None),
        P("train", "tensor", None),
        P(None, "train", None),
        P(None, "train", None),
        P(None, "train", None),
    )
    out_specs = (P(None, "train", "tensor"),) + cores
    return jax.shard_map(body, mesh=mesh, in_specs=in_specs, out_specs=out_specs, check_vma=False)
```

```python
import jax
import jax.numpy as jnp
from jax import lax
from jax.experimental import pallas as pl
from jax.experimental.pallas import tpu as pltpu
from jax.sharding import PartitionSpec as P

MESH = pl.DeviceIdType.MESH
BF16 = jnp.bfloat16
F32 = jnp.float32

BETA_ONE = 0.9
BETA_TWO = 0.999
LEARN_RATE = 0.01
WEIGHT_DECAY = 0.1
EPSILON = 1e-08
STEP_NUMBER = 10.0

VMEM_LIMIT = 48 * 1024 * 1024


def adamw_update(value_now, gradient, first_moment, second_moment):
    first_next = BETA_ONE * first_moment + (1.0 - BETA_ONE) * gradient
    second_next = BETA_TWO * second_moment + (1.0 - BETA_TWO) * gradient * gradient
    first_scale = 1.0 - BETA_ONE**STEP_NUMBER
    second_scale = 1.0 - BETA_TWO**STEP_NUMBER
    update = first_next / first_scale / (jnp.sqrt(second_next / second_scale) + EPSILON)
    value_next = value_now - LEARN_RATE * (update + WEIGHT_DECAY * value_now)
    return (value_next, first_next, second_next)


class Place:
    def __init__(self):
        self.train = lax.axis_index("train")
        self.tensor = lax.axis_index("tensor")
        self.core = self.train % 2
        self.y = (self.train // 2) % 4
        self.z_lo = self.train // 8
        self.x = self.tensor % 4
        self.z_hi = self.tensor // 4
        self.z = self.z_hi * 8 + self.z_lo

    def at_z(self, z):
        z = (z + 16) % 16
        return ((z % 8) * 8 + self.y * 2 + self.core, (z // 8) * 4 + self.x)

    def at_y(self, y):
        return (self.z_lo * 8 + ((y + 4) % 4) * 2 + self.core, self.tensor)

    def at_x(self, x):
        return (self.train, self.z_hi * 4 + (x + 4) % 4)

    def twin(self):
        return (self.train + 1 - 2 * self.core, self.tensor)

    def other_half(self):
        return (self.train, (1 - self.z_hi) * 4 + self.x)


def push(src, dst, sems, index, device):
    copy = pltpu.make_async_remote_copy(
        src_ref=src,
        dst_ref=dst,
        send_sem=sems.at[0, index],
        recv_sem=sems.at[1, index],
        device_id=device,
        device_id_type=MESH,
    )
    copy.start()
    return copy


def signal(device):
    pl.semaphore_signal(
        pltpu.get_barrier_semaphore(), inc=1, device_id=device, device_id_type=MESH
    )


def dma_sems(count):
    return pltpu.SemaphoreType.DMA((2, count))


def iota(shape, dim):
    return lax.broadcasted_iota(jnp.int32, shape, dim)


def one_hot(condition):
    return jnp.where(condition, 1.0, 0.0).astype(BF16)


def contract_first(left, right):
    return lax.dot_general(left, right, (((0,), (0,)), ((), ())), preferred_element_type=F32)


def add_blocks(dst, count, *terms):
    @pl.loop(0, count)
    def _(i):
        total = terms[0](i).astype(F32)
        for term in terms[1:]:
            total = total + term(i).astype(F32)
        dst[i] = total.astype(BF16)


def layer_kernel(
    up, down, rows, message, out,
    up_all, down_all, relay, rows_all, message_z, message_y, message_all,
    pick, combine, order_map, right_rows, right_all, left_all, weight, picked,
    part, hidden_far, hidden_near, hidden_pass, hidden,
    mixed, twin_in, sums, far, near, line, right_in, left_in, right_out, left_out,
    local_sem, z_sem, y_sem, far_sem, twin_sem, weight_sem, relay_sem,
    message_sem, spread_sem, hidden_sem, gather_sem,
    core_sem, mix_far_sem, mix_near_sem, right_sem, left_sem,
):
    at = Place()
    tensor, x, y, z_lo, z, core = at.tensor, at.x, at.y, at.z_lo, at.z, at.core
    twin = at.twin()
    x_right, x_left = at.at_x(x + 1), at.at_x(x - 1)
    y_right, y_left = at.at_y(y + 1), at.at_y(y - 1)
    z_right, z_left = at.at_z(z + 1), at.at_z(z - 1)

    def same_half(step):
        return (((z_lo + step) % 8) * 8 + y * 2 + core, tensor)

    for step in range(1, 8):
        signal(same_half(step))
    for step in (1, 2, 3):
        signal(at.at_x(x + step))
        signal(at.at_y(y + step))
    for device in (twin, z_right, z_left, at.other_half()):
        signal(device)
    pl.semaphore_wait(pltpu.get_barrier_semaphore(), 17)

    unsent = []

    def send(src, dst, sems, index, device):
        copy = push(src, dst, sems, index, device)
        unsent.append(copy)
        return copy

    def move(src, dst, index):
        copy = pltpu.make_async_copy(src, dst, local_sem.at[index])
        copy.start()
        return copy

    here = rows_all.at[z_lo, y, core]
    z_rights = [send(rows, here, z_sem, 0, z_right)]
    z_lefts = [send(rows, here, z_sem, 4, z_left)]

    moved_z = move(message.at[z_lo], message_z.at[z_lo], 0)
    by_z = [
        send(message.at[(z_lo + step) % 8], message_z.at[z_lo], message_sem, step, same_half(step))
        for step in range(1, 8)
    ]
    y_rights = [send(rows, here, y_sem, 0, y_right)]
    y_lefts = [send(rows, here, y_sem, 8, y_left)]
    moved_rows = move(rows, here, 1)

    weights = ((up, up_all), (down, down_all))

    def columns_of(half, to):
        return pl.ds(pl.multiple_of((half * 4 + to) * 512, 512), 512)

    def send_weight(w):
        origin, dst = weights[w]
        first, direct = [], []
        for way, device in ((0, x_right), (1, x_left)):
            first.append(
                send(origin.at[:, columns_of(way, (x + 2) % 4)], relay.at[w, way],
                     relay_sem, w * 2 + way, device)
            )
        for way, device, to in ((0, x_right, (x + 1) % 4), (1, x_left, (x + 3) % 4)):
            for half in (0, 1):
                direct.append(
                    send(origin.at[:, columns_of(half, to)], dst.at[half, x],
                         weight_sem, w * 4 + way * 2 + half, device)
                )
        for half in (0, 1):
            direct.append(move(origin.at[:, columns_of(half, x)], dst.at[half, x], 2 + w * 2 + half))
        return first, direct

    def pass_weight(w, first, direct):
        dst = weights[w][1]
        for way, device, source in ((0, x_right, (x + 3) % 4), (1, x_left, (x + 1) % 4)):
            first[way].wait_recv()
            direct.append(
                send(relay.at[w, way], dst.at[way, source], relay_sem, 4 + w * 2 + way, device)
            )

    def arrive(copies, own=()):
        for copy in copies:
            copy.wait_recv()
        for copy in own:
            copy.wait()

    up_first, up_direct = send_weight(0)

    blocks = [z_lo]
    for order in range(1, 8):
        step = (order + 1) // 2
        if order % 2 == 1:
            z_rights[step - 1].wait_recv()
            block = (z_lo - step + 8) % 8
            here = rows_all.at[block, y, core]
            if step < 4:
                z_rights.append(send(here, here, z_sem, step, z_right))
        else:
            z_lefts[step - 1].wait_recv()
            block = (z_lo + step) % 8
            here = rows_all.at[block, y, core]
            if step < 3:
                z_lefts.append(send(here, here, z_sem, 4 + step, z_left))
        blocks.append(block)
        y_rights.append(send(here, here, y_sem, order, y_right))
        y_lefts.append(send(here, here, y_sem, 8 + order, y_left))
        if order == 3:
            arrive(by_z, [moved_z])
            moved_y = move(message_z.at[:, y], message_y.at[:, y], 6)
            by_y = [
                send(message_z.at[:, (y + step) % 4], message_y.at[:, y],
                     message_sem, 7 + step, at.at_y(y + step))
                for step in (1, 2, 3)
            ]
        if order == 5:
            arrive(by_y, [moved_y])
            moved_core = move(message_y.at[:, :, core], message_all.at[tensor, :, :, core], 7)
            by_core = send(message_y.at[:, :, 1 - core], message_all.at[tensor, :, :, core],
                           message_sem, 0, twin)

    arrive([by_core], [moved_core])
    here = message_all.at[tensor]
    across = send(here, here, spread_sem, 0, at.other_half())
    spread = [send(here, here, spread_sem, step, at.at_x(x + step)) for step in (1, 2, 3)]

    far_copies, twin_copies = [], []

    def pass_rows(order):
        block = blocks[order]
        arrive([y_rights[order], y_lefts[order]])
        if order % 2 == 0:
            here, device = rows_all.at[block, (y + 3) % 4, core], y_right
        else:
            here, device = rows_all.at[block, (y + 1) % 4, core], y_left
        far_copies.append(send(here, here, far_sem, order, device))

    def twin_rows(order):
        far_copies[order].wait_recv()
        here = rows_all.at[blocks[order], :, core]
        twin_copies.append(send(here, here, twin_sem, order, twin))

    for order in range(4):
        pass_rows(order)
    pass_weight(0, up_first, up_direct)
    across.wait_recv()
    here = message_all.at[(1 - at.z_hi) * 4 + x]
    spread += [send(here, here, spread_sem, 3 + step, at.at_x(x + step)) for step in (1, 2, 3)]
    moved_rows.wait()
    for order in range(4, 8):
        pass_rows(order)
        twin_rows(order - 4)

    own = message_all[tensor].reshape(64, 2, 128)[:, 0, :].astype(BF16)
    tiled = []
    for first in (64, 96):
        tile = one_hot(iota((128, 256), 0) == first + iota((128, 256), 1) % 32)
        value = jnp.dot(own, tile, preferred_element_type=F32)
        keep = iota((64, 256), 1) // 32 == iota((64, 256), 0) % 8
        tiled.append(jnp.where(keep, value, 0.0).astype(BF16))

    @pl.loop(0, 8)
    def _(group):
        expand = one_hot(iota((64, 64), 1) == group * 8 + iota((64, 64), 0) // 8)
        slot, gate = (jnp.dot(expand, value, preferred_element_type=F32) for value in tiled)
        places, slots = iota((64, 256), 1), iota((64, 256), 0)
        match = (slot == (slots % 2 + 1).astype(F32)) & ((places // 8) % 4 == (slots // 2) % 4)
        pick[group] = one_hot(match)
        combine[group] = jnp.where(match, gate, 0.0).astype(BF16)

    for rr in range(2):
        for c in range(3):
            for b in range(4):
                k, n = iota((128, 128), 0), iota((128, 128), 1)
                here = (k - rr * 48 + b * 48 == c * 64 + n % 64) & (k >= rr * 48) & (k < rr * 48 + 48)
                order_map[b * 128 : b * 128 + 128, (rr * 3 + c) * 128 : (rr * 3 + c) * 128 + 128] = (
                    one_hot(here)
                )
    for order in range(4, 8):
        twin_rows(order)
    arrive(spread)

    @pl.loop(0, 8)
    def _(t):
        right_rows[...] = message_all[t].reshape(64, 2, 128)[:, 1, :]
        entries = jnp.concatenate(
            [right_rows[pl.ds(b, 16, stride=4), :] for b in range(4)], axis=1
        ).astype(BF16)
        placed = jnp.dot(entries, order_map[...], preferred_element_type=F32)
        for rr in range(2):
            for c in range(3):
                lanes = slice((rr * 3 + c) * 128, (rr * 3 + c) * 128 + 128)
                right_all[t * 2 + rr, pl.ds(c, 16, stride=3), :] = placed[:, lanes]

    arrive(up_direct[:4] + up_direct[6:], up_direct[4:6])
    down_first, down_direct = send_weight(1)

    widen = jnp.where(iota((8, 512), 1) // 64 == iota((8, 512), 0), 1.0, 0.0)

    @pl.loop(0, 8)
    def _(index):
        group, half = index // 2, index % 2
        left = message_all[at.z_hi * 4 + group, half * 4 + x].reshape(8, 2, 128)[:, 0, :]
        left_all[...] = contract_first(left, widen)
        for j in range(4):
            for lane in range(4):
                lanes = slice(lane * 128, lane * 128 + 128)
                delta = jnp.zeros((48, 128), F32)
                for r in range(16):
                    delta = delta + right_all[r] * left_all[j * 16 + r : j * 16 + r + 1, lanes]
                units = slice(j * 48, j * 48 + 48)
                weight[group, half, units, lanes] = (
                    up_all[half, group, units, lanes].astype(F32) + delta
                ).astype(BF16)

    pass_weight(1, down_first, down_direct)
    for order, block in enumerate(blocks):
        twin_copies[order].wait_recv()
    for group in range(8):
        value = jnp.dot(
            pick[group], rows_all[group].reshape(256, 1024), preferred_element_type=F32
        )
        picked[group * 64 : group * 64 + 64] = value.astype(BF16)

    def project(group):
        total = jnp.zeros((192, 512), F32)
        for half in (0, 1):
            total = total + lax.dot_general(
                weight[group, half], picked[:, half * 512 : half * 512 + 512],
                (((1,), (1,)), ((), ())), preferred_element_type=F32,
            )
        part[group] = total.astype(BF16)

    right_x, left_x, far_x = (x + 1) % 4, (x + 3) % 4, (x + 2) % 4
    top, low = pl.ds(0, 96), pl.ds(96, 96)
    project(far_x)
    copies = [
        send(part.at[far_x, top], hidden_far.at[0], hidden_sem, 0, x_right),
        send(part.at[far_x, low], hidden_far.at[1], hidden_sem, 1, x_left),
    ]
    project(right_x)
    copies.append(send(part.at[right_x, low], hidden_near.at[0, low], hidden_sem, 2, x_right))
    project(left_x)
    copies.append(send(part.at[left_x, top], hidden_near.at[1, top], hidden_sem, 3, x_left))
    copies[0].wait_recv()
    hidden_pass[0] = (part[right_x, top].astype(F32) + hidden_far[0].astype(F32)).astype(BF16)
    copies.append(send(hidden_pass.at[0], hidden_near.at[0, top], hidden_sem, 4, x_right))
    copies[1].wait_recv()
    hidden_pass[1] = (part[left_x, low].astype(F32) + hidden_far[1].astype(F32)).astype(BF16)
    copies.append(send(hidden_pass.at[1], hidden_near.at[1, low], hidden_sem, 5, x_left))
    project(x)
    arrive(copies[2:])
    value = part[x].astype(F32) + hidden_near[0].astype(F32) + hidden_near[1].astype(F32)
    hidden[x] = (value / (1.0 + jnp.exp(-value))).astype(BF16)
    here = hidden.at[x]
    from_left = send(here, here, gather_sem, 0, x_right)
    from_right = send(here, here, gather_sem, 1, x_left)
    from_left.wait_recv()
    here = hidden.at[left_x, top]
    far_top = send(here, here, gather_sem, 2, x_right)
    from_right.wait_recv()
    here = hidden.at[right_x, low]
    far_low = send(here, here, gather_sem, 3, x_left)
    arrive(down_direct[:4] + down_direct[6:], down_direct[4:6])
    arrive([far_top, far_low])

    order = [(y + 2) % 4, (y + 1) % 4, (y + 3) % 4, y]
    twins = {}
    for half in (0, 1):
        result = contract_first(
            hidden[...].reshape(768, 512), down_all[half].reshape(768, 512)
        ).astype(BF16)
        for group in range(8):
            value = contract_first(
                combine[group], result[group * 64 : group * 64 + 64]
            ).astype(BF16)
            for to_y in range(4):
                for to_core in range(2):
                    first = (to_y * 2 + to_core) * 32
                    mixed[to_core, to_y, half * 8 + group] = value[first : first + 32]
        zs = pl.ds(half * 8, 8)
        for i, to in enumerate(order):
            twins[i, half] = send(mixed.at[1 - core, to, zs], twin_in.at[to, zs],
                                  core_sem, half * 4 + i, twin)

    def sum_cores(i, half):
        to, base = order[i], half * 8
        twins[i, half].wait_recv()
        add_blocks(
            sums.at[i, pl.ds(base, 8)], 8,
            lambda k: mixed[core, to, base + k], lambda k: twin_in[to, base + k],
        )

    top, low = pl.ds(0, 8), pl.ds(8, 8)
    sum_cores(0, 0)
    copies = [send(sums.at[0, top], far.at[0], mix_far_sem, 0, y_right)]
    sum_cores(0, 1)
    copies.append(send(sums.at[0, low], far.at[1], mix_far_sem, 1, y_left))
    sum_cores(1, 1)
    copies.append(send(sums.at[1, low], near.at[0, low], mix_near_sem, 0, y_right))
    sum_cores(2, 0)
    copies.append(send(sums.at[2, top], near.at[1, top], mix_near_sem, 1, y_left))
    sum_cores(1, 0)
    sum_cores(2, 1)
    copies[0].wait_recv()
    add_blocks(sums.at[1], 8, lambda k: sums[1, k], lambda k: far[0, k])
    copies.append(send(sums.at[1, top], near.at[0, top], mix_near_sem, 2, y_right))
    copies[1].wait_recv()
    add_blocks(sums.at[2, low], 8, lambda k: sums[2, 8 + k], lambda k: far[1, k])
    copies.append(send(sums.at[2, low], near.at[1, low], mix_near_sem, 3, y_left))
    sum_cores(3, 0)
    sum_cores(3, 1)
    arrive(copies[2:])
    add_blocks(line, 16, lambda k: sums[3, k], lambda k: near[0, k], lambda k: near[1, k])

    rights, lefts = [], []
    for step in range(8):
        value = line[(z + 8 - step) % 16].astype(F32)
        if step > 0:
            rights[step - 1].wait_recv()
            value = value + right_in[step - 1].astype(F32)
        right_out[step] = value.astype(BF16)
        rights.append(send(right_out.at[step], right_in.at[step], right_sem, step, z_right))
        if step < 7:
            value = line[(z + 9 + step) % 16].astype(F32)
            if step > 0:
                lefts[step - 1].wait_recv()
                value = value + left_in[step - 1].astype(F32)
            left_out[step] = value.astype(BF16)
            lefts.append(send(left_out.at[step], left_in.at[step], left_sem, step, z_left))
    lefts[6].wait_recv()
    rights[7].wait_recv()
    value = line[z].astype(F32) + right_in[7].astype(F32) + left_in[6].astype(F32)
    out[...] = value.astype(BF16)
    for copy in unsent:
        copy.wait_send()


def layer(up, down, rows, message):
    any_space = pl.BlockSpec(memory_space=pl.ANY)
    return pl.pallas_call(
        layer_kernel,
        out_shape=jax.ShapeDtypeStruct((32, 512), BF16),
        in_specs=[any_space] * 4,
        out_specs=pl.BlockSpec(memory_space=pltpu.VMEM),
        scratch_shapes=[
            pltpu.VMEM((2, 4, 192, 512), BF16),
            pltpu.VMEM((2, 4, 192, 512), BF16),
            pltpu.VMEM((2, 2, 192, 512), BF16),
            pltpu.VMEM((8, 4, 2, 32, 1024), BF16),
            pltpu.VMEM((8, 4, 2, 2, 128), F32),
            pltpu.VMEM((8, 4, 2, 2, 128), F32),
            pltpu.VMEM((8, 8, 4, 2, 2, 128), F32),
            pltpu.VMEM((8, 64, 256), BF16),
            pltpu.VMEM((8, 64, 256), BF16),
            pltpu.VMEM((512, 768), BF16),
            pltpu.VMEM((64, 128), F32),
            pltpu.VMEM((16, 48, 128), F32),
            pltpu.VMEM((128, 512), F32),
            pltpu.VMEM((4, 2, 192, 512), BF16),
            pltpu.VMEM((512, 1024), BF16),
            pltpu.VMEM((4, 192, 512), BF16),
            pltpu.VMEM((2, 96, 512), BF16),
            pltpu.VMEM((2, 192, 512), BF16),
            pltpu.VMEM((2, 96, 512), BF16),
            pltpu.VMEM((4, 192, 512), BF16),
            pltpu.VMEM((2, 4, 16, 32, 512), BF16),
            pltpu.VMEM((4, 16, 32, 512), BF16),
            pltpu.VMEM((4, 16, 32, 512), BF16),
            pltpu.VMEM((2, 8, 32, 512), BF16),
            pltpu.VMEM((2, 16, 32, 512), BF16),
            pltpu.VMEM((16, 32, 512), BF16),
            pltpu.VMEM((8, 32, 512), BF16),
            pltpu.VMEM((7, 32, 512), BF16),
            pltpu.VMEM((8, 32, 512), BF16),
            pltpu.VMEM((7, 32, 512), BF16),
            pltpu.SemaphoreType.DMA((8,)),
            dma_sems(7),
            dma_sems(16),
            dma_sems(8),
            dma_sems(8),
            dma_sems(8),
            dma_sems(8),
            dma_sems(11),
            dma_sems(7),
            dma_sems(6),
            dma_sems(4),
            dma_sems(8),
            dma_sems(2),
            dma_sems(4),
            dma_sems(8),
            dma_sems(7),
        ],
        compiler_params=pltpu.CompilerParams(
            collective_id=0, has_side_effects=True, vmem_limit_bytes=VMEM_LIMIT
        ),
        name="layer",
    )(up, down, rows, message)


def body(
    core_left,
    core_right,
    grad_left,
    grad_right,
    first_left,
    first_right,
    second_left,
    second_right,
    up_base,
    down_base,
    states,
    routes,
    gates,
):
    left_next, first_left_next, second_left_next = adamw_update(
        core_left, grad_left, first_left, second_left
    )
    right_next, first_right_next, second_right_next = adamw_update(
        core_right, grad_right, first_right, second_right
    )
    chosen = (routes[..., None] == jnp.arange(64, dtype=jnp.int32)).astype(F32)
    taken = jnp.sum(chosen, axis=2)
    weight = jnp.sum(chosen * gates[..., None], axis=2)
    earlier = jnp.cumsum(taken, axis=1) - taken
    slot = taken * (earlier + 1.0)
    message = jnp.concatenate(
        [
            lax.reduce_precision(left_next, 8, 7).reshape(64, 64),
            slot.reshape(32, 64),
            weight.reshape(32, 64),
            lax.reduce_precision(right_next, 8, 7).reshape(96, 64),
            jnp.zeros((32, 64), F32),
        ],
        axis=0,
    )
    message = message.T.reshape(8, 4, 2, 2, 128)
    x = lax.axis_index("tensor") % 4
    rows = lax.dynamic_index_in_dim(states.reshape(32, 2, 4, 512), x, 2, keepdims=False)
    mixed = layer(up_base[0], down_base[0], rows.reshape(32, 1024), message)
    mixed = mixed.reshape(4, 8, 512)
    return (
        mixed,
        left_next,
        right_next,
        first_left_next,
        first_right_next,
        second_left_next,
        second_right_next,
    )


def solution(mesh):
    cores = (P("tensor", "train"),) * 6
    in_specs = cores + (P("tensor", "train"),) * 2 + (
        P("train", "tensor", None),
        P("train", "tensor", None),
        P(None, "train", None),
        P(None, "train", None),
        P(None, "train", None),
    )
    out_specs = (P(None, "train", "tensor"),) + cores
    return jax.shard_map(body, mesh=mesh, in_specs=in_specs, out_specs=out_specs, check_vma=False)
```

```python
import jax
import jax.numpy as jnp
from jax import lax
from jax.experimental import pallas as pl
from jax.experimental.pallas import tpu as pltpu
from jax.sharding import PartitionSpec as P

MESH = pl.DeviceIdType.MESH
BF16 = jnp.bfloat16
F32 = jnp.float32

BETA_ONE = 0.9
BETA_TWO = 0.999
LEARN_RATE = 0.01
WEIGHT_DECAY = 0.1
EPSILON = 1e-08
STEP_NUMBER = 10.0

VMEM_LIMIT = 60 * 1024 * 1024


def adamw_update(value_now, gradient, first_moment, second_moment):
    first_next = BETA_ONE * first_moment + (1.0 - BETA_ONE) * gradient
    second_next = BETA_TWO * second_moment + (1.0 - BETA_TWO) * gradient * gradient
    first_scale = 1.0 - BETA_ONE**STEP_NUMBER
    second_scale = 1.0 - BETA_TWO**STEP_NUMBER
    update = first_next / first_scale / (jnp.sqrt(second_next / second_scale) + EPSILON)
    value_next = value_now - LEARN_RATE * (update + WEIGHT_DECAY * value_now)
    return (value_next, first_next, second_next)


class Place:
    def __init__(self):
        self.train = lax.axis_index("train")
        self.tensor = lax.axis_index("tensor")
        self.core = self.train % 2
        self.y = (self.train // 2) % 4
        self.z_lo = self.train // 8
        self.x = self.tensor % 4
        self.z_hi = self.tensor // 4
        self.z = self.z_hi * 8 + self.z_lo

    def at_z(self, z):
        z = (z + 16) % 16
        return ((z % 8) * 8 + self.y * 2 + self.core, (z // 8) * 4 + self.x)

    def at_y(self, y):
        return (self.z_lo * 8 + ((y + 4) % 4) * 2 + self.core, self.tensor)

    def at_x(self, x):
        return (self.train, self.z_hi * 4 + (x + 4) % 4)

    def twin(self):
        return (self.train + 1 - 2 * self.core, self.tensor)

    def other_half(self):
        return (self.train, (1 - self.z_hi) * 4 + self.x)


def push(src, dst, sems, index, device):
    copy = pltpu.make_async_remote_copy(
        src_ref=src,
        dst_ref=dst,
        send_sem=sems.at[0, index],
        recv_sem=sems.at[1, index],
        device_id=device,
        device_id_type=MESH,
    )
    copy.start()
    return copy


def signal(device):
    pl.semaphore_signal(
        pltpu.get_barrier_semaphore(), inc=1, device_id=device, device_id_type=MESH
    )


def dma_sems(count):
    return pltpu.SemaphoreType.DMA((2, count))


def iota(shape, dim):
    return lax.broadcasted_iota(jnp.int32, shape, dim)


def one_hot(condition):
    return jnp.where(condition, 1.0, 0.0).astype(BF16)


def contract_first(left, right):
    return lax.dot_general(left, right, (((0,), (0,)), ((), ())), preferred_element_type=F32)


def layer_kernel(
    up, down, rows, message, out,
    up_all, down_all, relay, rows_all, message_z, message_y, message_all,
    pick, combine, order_map, right_rows, entries, right_all, left_all, weight, picked,
    part, hidden_far, hidden_near, hidden_pass, hidden,
    result, twin_in, slots_in, slots_relay, line, right_in, left_in, right_out, left_out,
    local_sem, z_sem, y_sem, far_sem, twin_sem, weight_sem, relay_sem,
    message_sem, spread_sem, hidden_sem, gather_sem,
    core_sem, slots_sem, slots_relay_sem, right_sem, left_sem,
):
    at = Place()
    tensor, x, y, z_lo, z, core = at.tensor, at.x, at.y, at.z_lo, at.z, at.core
    twin = at.twin()
    x_right, x_left = at.at_x(x + 1), at.at_x(x - 1)
    y_right, y_left = at.at_y(y + 1), at.at_y(y - 1)
    z_right, z_left = at.at_z(z + 1), at.at_z(z - 1)

    def same_half(step):
        return (((z_lo + step) % 8) * 8 + y * 2 + core, tensor)

    for step in range(1, 8):
        signal(same_half(step))
    for step in (1, 2, 3):
        signal(at.at_x(x + step))
        signal(at.at_y(y + step))
    for device in (twin, z_right, z_left, at.other_half()):
        signal(device)
    pl.semaphore_wait(pltpu.get_barrier_semaphore(), 17)

    unsent = []

    def send(src, dst, sems, index, device):
        copy = push(src, dst, sems, index, device)
        unsent.append(copy)
        return copy

    def move(src, dst, index):
        copy = pltpu.make_async_copy(src, dst, local_sem.at[index])
        copy.start()
        return copy

    here = rows_all.at[z_lo, y, core]
    z_rights = [send(rows, here, z_sem, 0, z_right)]
    z_lefts = [send(rows, here, z_sem, 4, z_left)]

    moved_z = move(message.at[z_lo], message_z.at[z_lo], 0)
    by_z = [
        send(message.at[(z_lo + step) % 8], message_z.at[z_lo], message_sem, step, same_half(step))
        for step in range(1, 8)
    ]
    y_rights = [send(rows, here, y_sem, 0, y_right)]
    y_lefts = [send(rows, here, y_sem, 8, y_left)]
    moved_rows = move(rows, here, 1)

    weights = ((up, up_all), (down, down_all))

    def columns_of(half, to):
        return pl.ds(pl.multiple_of((half * 4 + to) * 512, 512), 512)

    def send_weight(w):
        origin, dst = weights[w]
        first, direct = [], []
        for way, device in ((0, x_right), (1, x_left)):
            first.append(
                send(origin.at[:, columns_of(way, (x + 2) % 4)], relay.at[w, way],
                     relay_sem, w * 2 + way, device)
            )
        for way, device, to in ((0, x_right, (x + 1) % 4), (1, x_left, (x + 3) % 4)):
            for half in (0, 1):
                direct.append(
                    send(origin.at[:, columns_of(half, to)], dst.at[half, x],
                         weight_sem, w * 4 + way * 2 + half, device)
                )
        for half in (0, 1):
            direct.append(move(origin.at[:, columns_of(half, x)], dst.at[half, x], 2 + w * 2 + half))
        return first, direct

    def pass_weight(w, first, direct):
        dst = weights[w][1]
        for way, device, source in ((0, x_right, (x + 3) % 4), (1, x_left, (x + 1) % 4)):
            first[way].wait_recv()
            direct.append(
                send(relay.at[w, way], dst.at[way, source], relay_sem, 4 + w * 2 + way, device)
            )

    def arrive(copies, own=()):
        for copy in copies:
            copy.wait_recv()
        for copy in own:
            copy.wait()

    up_first, up_direct = send_weight(0)

    blocks = [z_lo]
    for order in range(1, 8):
        step = (order + 1) // 2
        if order % 2 == 1:
            z_rights[step - 1].wait_recv()
            block = (z_lo - step + 8) % 8
            here = rows_all.at[block, y, core]
            if step < 4:
                z_rights.append(send(here, here, z_sem, step, z_right))
        else:
            z_lefts[step - 1].wait_recv()
            block = (z_lo + step) % 8
            here = rows_all.at[block, y, core]
            if step < 3:
                z_lefts.append(send(here, here, z_sem, 4 + step, z_left))
        blocks.append(block)
        y_rights.append(send(here, here, y_sem, order, y_right))
        y_lefts.append(send(here, here, y_sem, 8 + order, y_left))
        if order == 3:
            arrive(by_z, [moved_z])
            moved_y = move(message_z.at[:, y], message_y.at[:, y], 6)
            by_y = [
                send(message_z.at[:, (y + step) % 4], message_y.at[:, y],
                     message_sem, 7 + step, at.at_y(y + step))
                for step in (1, 2, 3)
            ]
        if order == 5:
            arrive(by_y, [moved_y])
            moved_core = move(message_y.at[:, :, core], message_all.at[tensor, :, :, core], 7)
            by_core = send(message_y.at[:, :, 1 - core], message_all.at[tensor, :, :, core],
                           message_sem, 0, twin)

    arrive([by_core], [moved_core])
    here = message_all.at[tensor]
    across = send(here, here, spread_sem, 0, at.other_half())
    spread = [send(here, here, spread_sem, step, at.at_x(x + step)) for step in (1, 2, 3)]

    far_copies, twin_copies = [], []

    def pass_rows(order):
        block = blocks[order]
        arrive([y_rights[order], y_lefts[order]])
        if order % 2 == 0:
            here, device = rows_all.at[block, (y + 3) % 4, core], y_right
        else:
            here, device = rows_all.at[block, (y + 1) % 4, core], y_left
        far_copies.append(send(here, here, far_sem, order, device))

    def twin_rows(order):
        far_copies[order].wait_recv()
        here = rows_all.at[blocks[order], :, core]
        twin_copies.append(send(here, here, twin_sem, order, twin))

    for order in range(4):
        pass_rows(order)
    pass_weight(0, up_first, up_direct)
    across.wait_recv()
    here = message_all.at[(1 - at.z_hi) * 4 + x]
    spread += [send(here, here, spread_sem, 3 + step, at.at_x(x + step)) for step in (1, 2, 3)]
    down_first, down_direct = send_weight(1)
    moved_rows.wait()
    for order in range(4, 8):
        pass_rows(order)
        twin_rows(order - 4)

    def spread_rows(messages, first, count):
        tile = one_hot(iota((128, count), 0) == first + iota((128, count), 1) % 32)
        return jnp.dot(messages, tile, preferred_element_type=F32).astype(BF16)

    own = message_all[tensor].reshape(64, 2, 128)[:, 0, :].astype(BF16)
    codes = spread_rows(own, 64, 512)

    @pl.loop(0, 4)
    def _(pair):
        slots, source = iota((128, 64), 0), iota((128, 64), 1)
        expand = one_hot(source == (pair * 2 + (slots // 8) % 2) * 8 + slots // 16)
        code = jnp.dot(expand, codes, preferred_element_type=F32)
        slots, places = iota((128, 512), 0), iota((128, 512), 1)
        match = (
            (code == (slots % 2 + 1).astype(F32))
            & (places // 256 == (slots // 8) % 2)
            & ((places // 32) % 8 == slots // 16)
            & ((places // 8) % 4 == (slots // 2) % 4)
        )
        pick[pair] = one_hot(match)

    passed = message_z[...].reshape(64, 2, 128)[:, 0, :].astype(BF16)
    codes, gates = spread_rows(passed, 64, 256), spread_rows(passed, 96, 256)

    @pl.loop(0, 8)
    def _(expert):
        slots, source = iota((64, 64), 0), iota((64, 64), 1)
        expand = one_hot(source == (slots // 8) * 8 + expert)
        code = jnp.dot(expand, codes, preferred_element_type=F32)
        gate = jnp.dot(expand, gates, preferred_element_type=F32)
        slots, places = iota((64, 256), 0), iota((64, 256), 1)
        match = (
            (code == (slots % 2 + 1).astype(F32))
            & (places // 32 == slots // 8)
            & ((places // 8) % 4 == (slots // 2) % 4)
        )
        combine[expert] = jnp.where(match, gate, 0.0).astype(BF16)

    for rr in range(2):
        for c in range(3):
            for b in range(4):
                k, n = iota((128, 128), 0), iota((128, 128), 1)
                here = (k - rr * 48 + b * 48 == c * 64 + n % 64) & (k >= rr * 48) & (k < rr * 48 + 48)
                order_map[b * 128 : b * 128 + 128, (rr * 3 + c) * 128 : (rr * 3 + c) * 128 + 128] = (
                    one_hot(here)
                )
    for order in range(4, 8):
        twin_rows(order)
    arrive(spread)

    for t in range(8):
        right_rows[t] = message_all[t].reshape(64, 2, 128)[:, 1, :]
        entries[t * 16 : t * 16 + 16] = jnp.concatenate(
            [right_rows[t, pl.ds(b, 16, stride=4), :] for b in range(4)], axis=1
        ).astype(BF16)
    placed = jnp.dot(entries[...], order_map[...], preferred_element_type=F32)
    for t in range(8):
        for rr in range(2):
            for c in range(3):
                lanes = slice((rr * 3 + c) * 128, (rr * 3 + c) * 128 + 128)
                right_all[t * 2 + rr, pl.ds(c, 16, stride=3), :] = (
                    placed[t * 16 : t * 16 + 16, lanes]
                )

    arrive(up_direct[:4] + up_direct[6:], up_direct[4:6])

    widen = jnp.where(iota((8, 512), 1) // 64 == iota((8, 512), 0), 1.0, 0.0)

    @pl.loop(0, 8)
    def _(index):
        group, half = index // 2, index % 2
        left = message_all[at.z_hi * 4 + group, half * 4 + x].reshape(8, 2, 128)[:, 0, :]
        left_all[...] = contract_first(left, widen)
        for j in range(4):
            for lane in range(4):
                lanes = slice(lane * 128, lane * 128 + 128)
                delta = jnp.zeros((48, 128), F32)
                for r in range(16):
                    delta = delta + right_all[r] * left_all[j * 16 + r : j * 16 + r + 1, lanes]
                units = slice(j * 48, j * 48 + 48)
                weight[group, half, units, lanes] = (
                    up_all[half, group, units, lanes].astype(F32) + delta
                ).astype(BF16)

    pass_weight(1, down_first, down_direct)
    for order, block in enumerate(blocks):
        twin_copies[order].wait_recv()
    for pair in range(4):
        value = jnp.dot(
            pick[pair],
            rows_all[pair * 2 : pair * 2 + 2].reshape(512, 1024),
            preferred_element_type=F32,
        ).astype(BF16)
        for group in range(8):
            picked[pl.ds(group * 64 + pair * 16, 16), :] = value[group * 16 : group * 16 + 16]

    def project(group):
        total = jnp.zeros((192, 512), F32)
        for half in (0, 1):
            total = total + lax.dot_general(
                weight[group, half], picked[:, half * 512 : half * 512 + 512],
                (((1,), (1,)), ((), ())), preferred_element_type=F32,
            )
        part[group] = total.astype(BF16)

    right_x, left_x, far_x = (x + 1) % 4, (x + 3) % 4, (x + 2) % 4
    top, low = pl.ds(0, 96), pl.ds(96, 96)
    project(far_x)
    copies = [
        send(part.at[far_x, top], hidden_far.at[0], hidden_sem, 0, x_right),
        send(part.at[far_x, low], hidden_far.at[1], hidden_sem, 1, x_left),
    ]
    project(right_x)
    copies.append(send(part.at[right_x, low], hidden_near.at[0, low], hidden_sem, 2, x_right))
    project(left_x)
    copies.append(send(part.at[left_x, top], hidden_near.at[1, top], hidden_sem, 3, x_left))
    copies[0].wait_recv()
    hidden_pass[0] = (part[right_x, top].astype(F32) + hidden_far[0].astype(F32)).astype(BF16)
    copies.append(send(hidden_pass.at[0], hidden_near.at[0, top], hidden_sem, 4, x_right))
    copies[1].wait_recv()
    hidden_pass[1] = (part[left_x, low].astype(F32) + hidden_far[1].astype(F32)).astype(BF16)
    copies.append(send(hidden_pass.at[1], hidden_near.at[1, low], hidden_sem, 5, x_left))
    project(x)
    arrive(copies[2:])
    value = part[x].astype(F32) + hidden_near[0].astype(F32) + hidden_near[1].astype(F32)
    hidden[x] = (value / (1.0 + jnp.exp(-value))).astype(BF16)
    here = hidden.at[x]
    from_left = send(here, here, gather_sem, 0, x_right)
    from_right = send(here, here, gather_sem, 1, x_left)
    from_left.wait_recv()
    here = hidden.at[left_x, top]
    far_top = send(here, here, gather_sem, 2, x_right)
    from_right.wait_recv()
    here = hidden.at[right_x, low]
    far_low = send(here, here, gather_sem, 3, x_left)
    arrive(down_direct[:4] + down_direct[6:], down_direct[4:6])
    arrive([far_top, far_low])

    right_y, left_y, far_y = (y + 1) % 4, (y + 3) % 4, (y + 2) % 4
    twins, direct, relayed, own_slots = [], [], [], []
    for half in (0, 1):
        result[half] = (
            contract_first(hidden[...].reshape(768, 512), down_all[half].reshape(768, 512))
            .astype(BF16)
            .reshape(4, 2, 64, 512)
        )
        twins.append(send(result.at[half, :, 1 - core], twin_in.at[half], core_sem, half, twin))
        relayed.append(
            send(result.at[half, far_y, core], slots_relay.at[half, 0],
                 slots_relay_sem, half, y_right)
        )
        here = slots_in.at[half, y, core]
        direct.append(send(result.at[half, right_y, core], here, slots_sem, half * 2, y_right))
        direct.append(send(result.at[half, left_y, core], here, slots_sem, half * 2 + 1, y_left))
        own_slots.append(move(result.at[half, y, core], here, 8 + half))
    for half in (0, 1):
        twins[half].wait_recv()
        relayed.append(
            send(twin_in.at[half, far_y], slots_relay.at[half, 1],
                 slots_relay_sem, 2 + half, y_left)
        )
        here = slots_in.at[half, y, 1 - core]
        direct.append(send(twin_in.at[half, right_y], here, slots_sem, 4 + half * 2, y_right))
        direct.append(send(twin_in.at[half, left_y], here, slots_sem, 5 + half * 2, y_left))
        own_slots.append(move(twin_in.at[half, y], here, 10 + half))
    onward = []
    for half in (0, 1):
        relayed[half].wait_recv()
        onward.append(
            send(slots_relay.at[half, 0], slots_in.at[half, left_y, core],
                 slots_relay_sem, 4 + half, y_right)
        )
    for half in (0, 1):
        relayed[2 + half].wait_recv()
        onward.append(
            send(slots_relay.at[half, 1], slots_in.at[half, right_y, 1 - core],
                 slots_relay_sem, 6 + half, y_left)
        )
    for half in (0, 1):
        arrive(
            [direct[half * 2], direct[half * 2 + 1], direct[4 + half * 2], direct[5 + half * 2]]
            + [onward[half], onward[2 + half]],
            [own_slots[half], own_slots[2 + half]],
        )
        value = contract_first(
            combine[...].reshape(512, 256), slots_in[half].reshape(512, 512)
        )
        for group in range(8):
            line[half * 8 + group] = value[group * 32 : group * 32 + 32]

    rights, lefts = [], []
    for step in range(8):
        value = line[(z + 8 - step) % 16]
        if step > 0:
            rights[step - 1].wait_recv()
            value = value + right_in[step - 1].astype(F32)
        right_out[step] = value.astype(BF16)
        rights.append(send(right_out.at[step], right_in.at[step], right_sem, step, z_right))
        if step < 7:
            value = line[(z + 9 + step) % 16]
            if step > 0:
                lefts[step - 1].wait_recv()
                value = value + left_in[step - 1].astype(F32)
            left_out[step] = value.astype(BF16)
            lefts.append(send(left_out.at[step], left_in.at[step], left_sem, step, z_left))
    lefts[6].wait_recv()
    rights[7].wait_recv()
    value = line[z] + right_in[7].astype(F32) + left_in[6].astype(F32)
    out[...] = value.astype(BF16)
    for copy in unsent:
        copy.wait_send()


def layer(up, down, rows, message):
    any_space = pl.BlockSpec(memory_space=pl.ANY)
    return pl.pallas_call(
        layer_kernel,
        out_shape=jax.ShapeDtypeStruct((32, 512), BF16),
        in_specs=[any_space] * 4,
        out_specs=pl.BlockSpec(memory_space=pltpu.VMEM),
        scratch_shapes=[
            pltpu.VMEM((2, 4, 192, 512), BF16),
            pltpu.VMEM((2, 4, 192, 512), BF16),
            pltpu.VMEM((2, 2, 192, 512), BF16),
            pltpu.VMEM((8, 4, 2, 32, 1024), BF16),
            pltpu.VMEM((8, 4, 2, 2, 128), F32),
            pltpu.VMEM((8, 4, 2, 2, 128), F32),
            pltpu.VMEM((8, 8, 4, 2, 2, 128), F32),
            pltpu.VMEM((4, 128, 512), BF16),
            pltpu.VMEM((8, 64, 256), BF16),
            pltpu.VMEM((512, 768), BF16),
            pltpu.VMEM((8, 64, 128), F32),
            pltpu.VMEM((128, 512), BF16),
            pltpu.VMEM((16, 48, 128), F32),
            pltpu.VMEM((128, 512), F32),
            pltpu.VMEM((4, 2, 192, 512), BF16),
            pltpu.VMEM((512, 1024), BF16),
            pltpu.VMEM((4, 192, 512), BF16),
            pltpu.VMEM((2, 96, 512), BF16),
            pltpu.VMEM((2, 192, 512), BF16),
            pltpu.VMEM((2, 96, 512), BF16),
            pltpu.VMEM((4, 192, 512), BF16),
            pltpu.VMEM((2, 4, 2, 64, 512), BF16),
            pltpu.VMEM((2, 4, 64, 512), BF16),
            pltpu.VMEM((2, 4, 2, 64, 512), BF16),
            pltpu.VMEM((2, 2, 64, 512), BF16),
            pltpu.VMEM((16, 32, 512), F32),
            pltpu.VMEM((8, 32, 512), BF16),
            pltpu.VMEM((7, 32, 512), BF16),
            pltpu.VMEM((8, 32, 512), BF16),
            pltpu.VMEM((7, 32, 512), BF16),
            pltpu.SemaphoreType.DMA((12,)),
            dma_sems(7),
            dma_sems(16),
            dma_sems(8),
            dma_sems(8),
            dma_sems(8),
            dma_sems(8),
            dma_sems(11),
            dma_sems(7),
            dma_sems(6),
            dma_sems(4),
            dma_sems(2),
            dma_sems(8),
            dma_sems(8),
            dma_sems(8),
            dma_sems(7),
        ],
        compiler_params=pltpu.CompilerParams(
            collective_id=0, has_side_effects=True, vmem_limit_bytes=VMEM_LIMIT
        ),
        name="layer",
    )(up, down, rows, message)


def body(
    core_left,
    core_right,
    grad_left,
    grad_right,
    first_left,
    first_right,
    second_left,
    second_right,
    up_base,
    down_base,
    states,
    routes,
    gates,
):
    left_next, first_left_next, second_left_next = adamw_update(
        core_left, grad_left, first_left, second_left
    )
    right_next, first_right_next, second_right_next = adamw_update(
        core_right, grad_right, first_right, second_right
    )
    chosen = (routes[..., None] == jnp.arange(64, dtype=jnp.int32)).astype(F32)
    taken = jnp.sum(chosen, axis=2)
    weight = jnp.sum(chosen * gates[..., None], axis=2)
    earlier = jnp.cumsum(taken, axis=1) - taken
    slot = taken * (earlier + 1.0)
    message = jnp.concatenate(
        [
            lax.reduce_precision(left_next, 8, 7).reshape(64, 64),
            slot.reshape(32, 64),
            weight.reshape(32, 64),
            lax.reduce_precision(right_next, 8, 7).reshape(96, 64),
            jnp.zeros((32, 64), F32),
        ],
        axis=0,
    )
    message = message.T.reshape(8, 4, 2, 2, 128)
    x = lax.axis_index("tensor") % 4
    rows = lax.dynamic_index_in_dim(states.reshape(32, 2, 4, 512), x, 2, keepdims=False)
    mixed = layer(up_base[0], down_base[0], rows.reshape(32, 1024), message)
    mixed = mixed.reshape(4, 8, 512)
    return (
        mixed,
        left_next,
        right_next,
        first_left_next,
        first_right_next,
        second_left_next,
        second_right_next,
    )


def solution(mesh):
    cores = (P("tensor", "train"),) * 6
    in_specs = cores + (P("tensor", "train"),) * 2 + (
        P("train", "tensor", None),
        P("train", "tensor", None),
        P(None, "train", None),
        P(None, "train", None),
        P(None, "train", None),
    )
    out_specs = (P(None, "train", "tensor"),) + cores
    return jax.shard_map(body, mesh=mesh, in_specs=in_specs, out_specs=out_specs, check_vma=False)
```

```python
import jax
import jax.numpy as jnp
from jax import lax
from jax.experimental import pallas as pl
from jax.experimental.pallas import tpu as pltpu
from jax.sharding import PartitionSpec as P

MESH = pl.DeviceIdType.MESH
BF16 = jnp.bfloat16
F32 = jnp.float32

BETA_ONE = 0.9
BETA_TWO = 0.999
LEARN_RATE = 0.01
WEIGHT_DECAY = 0.1
EPSILON = 1e-08
STEP_NUMBER = 10.0

VMEM_LIMIT = 60 * 1024 * 1024


def adamw_update(value_now, gradient, first_moment, second_moment):
    first_next = BETA_ONE * first_moment + (1.0 - BETA_ONE) * gradient
    second_next = BETA_TWO * second_moment + (1.0 - BETA_TWO) * gradient * gradient
    first_scale = 1.0 - BETA_ONE**STEP_NUMBER
    second_scale = 1.0 - BETA_TWO**STEP_NUMBER
    update = first_next / first_scale / (jnp.sqrt(second_next / second_scale) + EPSILON)
    value_next = value_now - LEARN_RATE * (update + WEIGHT_DECAY * value_now)
    return (value_next, first_next, second_next)


def prepare_kernel(
    core_left, core_right, grad_left, grad_right, first_left, first_right, second_left, second_right,
    routes, gates,
    left_next, right_next, first_left_next, first_right_next, second_left_next, second_right_next,
    message, entries,
):
    left, first, second = adamw_update(
        core_left[...], grad_left[...], first_left[...], second_left[...]
    )
    left_next[...], first_left_next[...], second_left_next[...] = left, first, second
    right, first, second = adamw_update(
        core_right[...], grad_right[...], first_right[...], second_right[...]
    )
    right_next[...], first_right_next[...], second_right_next[...] = right, first, second

    for r in range(16):
        entries[0, r * 4 : r * 4 + 4] = left[:, r * 64 : r * 64 + 64]
    for pair in range(48):
        entries[1, pair * 2 : pair * 2 + 2] = right[:, pair * 64 : pair * 64 + 64]
    entries[1, 96:128] = jnp.zeros((32, 64), F32)
    expert = lax.broadcasted_iota(jnp.int32, (32, 64), 1)
    taken, weight = jnp.zeros((32, 64), F32), jnp.zeros((32, 64), F32)
    for k in range(8):
        chosen = routes[:, k : k + 1] == expert
        taken = taken + jnp.where(chosen, 1.0, 0.0)
        weight = weight + jnp.where(chosen, gates[:, k : k + 1], 0.0)
    to, by = (lax.broadcasted_iota(jnp.int32, (32, 32), dim) for dim in (0, 1))
    before = jnp.where((by < to) & (by // 8 == to // 8), 1.0, 0.0)
    earlier = jnp.dot(before, taken, preferred_element_type=F32)
    entries[0, 64:96] = taken * (earlier + 1.0)
    entries[0, 96:128] = weight
    row, column = (lax.broadcasted_iota(jnp.int32, (128, 128), dim) for dim in (0, 1))
    same = jnp.where(row == column, 1.0, 0.0).astype(BF16)
    for kind in range(2):
        message[:, kind, :] = lax.dot_general(
            entries[kind].astype(BF16), same, (((0,), (0,)), ((), ())), preferred_element_type=F32
        )


def prepare(cores, routes, gates):
    return pl.pallas_call(
        prepare_kernel,
        out_shape=(
            *(jax.ShapeDtypeStruct(shape, F32) for shape in ((4, 1024), (2, 3072)) * 3),
            jax.ShapeDtypeStruct((64, 2, 128), F32),
        ),
        scratch_shapes=[pltpu.VMEM((2, 128, 64), F32)],
        name="prepare",
    )(*cores, routes, gates)


class Place:
    def __init__(self):
        self.train = lax.axis_index("train")
        self.tensor = lax.axis_index("tensor")
        self.core = self.train % 2
        self.y = (self.train // 2) % 4
        self.z_lo = self.train // 8
        self.x = self.tensor % 4
        self.z_hi = self.tensor // 4
        self.z = self.z_hi * 8 + self.z_lo

    def at_z(self, z):
        z = (z + 16) % 16
        return ((z % 8) * 8 + self.y * 2 + self.core, (z // 8) * 4 + self.x)

    def at_y(self, y):
        return (self.z_lo * 8 + ((y + 4) % 4) * 2 + self.core, self.tensor)

    def at_x(self, x):
        return (self.train, self.z_hi * 4 + (x + 4) % 4)

    def across_y(self, y):
        return (self.z_lo * 8 + ((y + 4) % 4) * 2 + 1 - self.core, self.tensor)

    def twin(self):
        return (self.train + 1 - 2 * self.core, self.tensor)

    def other_half(self):
        return (self.train, (1 - self.z_hi) * 4 + self.x)


def push(src, dst, sems, index, device):
    copy = pltpu.make_async_remote_copy(
        src_ref=src,
        dst_ref=dst,
        send_sem=sems.at[0, index],
        recv_sem=sems.at[1, index],
        device_id=device,
        device_id_type=MESH,
    )
    copy.start()
    return copy


def signal(device):
    pl.semaphore_signal(
        pltpu.get_barrier_semaphore(), inc=1, device_id=device, device_id_type=MESH
    )


def dma_sems(count):
    return pltpu.SemaphoreType.DMA((2, count))


def iota(shape, dim):
    return lax.broadcasted_iota(jnp.int32, shape, dim)


def one_hot(condition):
    return jnp.where(condition, 1.0, 0.0).astype(BF16)


def contract_first(left, right):
    return lax.dot_general(left, right, (((0,), (0,)), ((), ())), preferred_element_type=F32)


def layer_kernel(
    up, down, rows, message, out,
    up_all, down_all, relay, rows_z, slots_out, rows_relay, message_z, message_y, message_all,
    pick, combine, order_map, right_rows, entries, right_all, left_all, weight, picked,
    part, hidden_far, hidden_near, hidden_pass, hidden,
    result, twin_in, slots_in, slots_relay, line, right_in, left_in, right_out, left_out,
    local_sem, z_sem, y_sem, rows_relay_sem, twin_sem, weight_sem, relay_sem,
    message_sem, spread_sem, hidden_sem, gather_sem,
    core_sem, slots_sem, slots_relay_sem, right_sem, left_sem,
):
    at = Place()
    tensor, x, y, z_lo, z, core = at.tensor, at.x, at.y, at.z_lo, at.z, at.core
    twin = at.twin()
    x_right, x_left = at.at_x(x + 1), at.at_x(x - 1)
    y_right, y_left = at.at_y(y + 1), at.at_y(y - 1)
    z_right, z_left = at.at_z(z + 1), at.at_z(z - 1)

    def same_half(step):
        return (((z_lo + step) % 8) * 8 + y * 2 + core, tensor)

    for step in range(1, 8):
        signal(same_half(step))
    for step in (1, 2, 3):
        signal(at.at_x(x + step))
        signal(at.at_y(y + step))
    for device in (twin, z_right, z_left, at.other_half()):
        signal(device)
    signal(at.across_y(y + 1))
    signal(at.across_y(y - 1))
    pl.semaphore_wait(pltpu.get_barrier_semaphore(), 19)

    unsent = []

    def send(src, dst, sems, index, device):
        copy = push(src, dst, sems, index, device)
        unsent.append(copy)
        return copy

    def move(src, dst, index):
        copy = pltpu.make_async_copy(src, dst, local_sem.at[index])
        copy.start()
        return copy

    def columns_of(half, to):
        return pl.ds(pl.multiple_of((half * 4 + to) * 512, 512), 512)

    halves = [
        (rows.at[:, columns_of(half, x)], pl.ds(half * 512, 512)) for half in (0, 1)
    ]
    z_rights, z_lefts = [], []
    for half, (origin, lanes) in enumerate(halves):
        z_rights.append(send(origin, rows_z.at[1, :, lanes], z_sem, half, z_right))
        z_lefts.append(send(origin, rows_z.at[2, :, lanes], z_sem, 2 + half, z_left))
    moved_rows = [
        move(origin, rows_z.at[0, :, lanes], half * 11 + 1)
        for half, (origin, lanes) in enumerate(halves)
    ]

    moved_z = move(message.at[z_lo], message_z.at[z_lo], 0)
    by_z = [
        send(message.at[(z_lo + step) % 8], message_z.at[z_lo], message_sem, step, same_half(step))
        for step in range(1, 8)
    ]

    weights = ((up, up_all), (down, down_all))

    def send_weight(w):
        origin, dst = weights[w]
        first, direct = [], []
        for way, device in ((0, x_right), (1, x_left)):
            first.append(
                send(origin.at[:, columns_of(way, (x + 2) % 4)], relay.at[w, way],
                     relay_sem, w * 2 + way, device)
            )
        for way, device, to in ((0, x_right, (x + 1) % 4), (1, x_left, (x + 3) % 4)):
            for half in (0, 1):
                direct.append(
                    send(origin.at[:, columns_of(half, to)], dst.at[half, x],
                         weight_sem, w * 4 + way * 2 + half, device)
                )
        for half in (0, 1):
            direct.append(move(origin.at[:, columns_of(half, x)], dst.at[half, x], 2 + w * 2 + half))
        return first, direct

    def pass_weight(w, first, direct):
        dst = weights[w][1]
        for way, device, source in ((0, x_right, (x + 3) % 4), (1, x_left, (x + 1) % 4)):
            first[way].wait_recv()
            direct.append(
                send(relay.at[w, way], dst.at[way, source], relay_sem, 4 + w * 2 + way, device)
            )

    def arrive(copies, own=()):
        for copy in copies:
            copy.wait_recv()
        for copy in own:
            copy.wait()

    up_first, up_direct = send_weight(0)

    blocks = [z_lo]
    for order in range(1, 8):
        step = (order + 1) // 2
        blocks.append((z_lo - step + 8) % 8 if order % 2 == 1 else (z_lo + step) % 8)

    def next_rows(order):
        if order == 1:
            arrive(z_rights[:2])
        elif order == 2:
            arrive(z_lefts[:2])
        elif order % 2 == 1:
            z_rights[order // 2 + 1].wait_recv()
        else:
            z_lefts[order // 2].wait_recv()
        here = rows_z.at[order]
        if order in (1, 3, 5):
            z_rights.append(send(here, rows_z.at[order + 2], z_sem, 3 + order, z_right))
        elif order in (2, 4):
            z_lefts.append(send(here, rows_z.at[order + 2], z_sem, 3 + order, z_left))

    right_y, left_y, far_y = (y + 1) % 4, (y + 3) % 4, (y + 2) % 4
    near_rows, twin_rows, rows_first, rows_onward, own_rows = [], [], [], [], []
    mine = y * 2 + core

    def send_rows(pair):
        value = jnp.dot(
            pick[pair],
            rows_z[pair * 2 : pair * 2 + 2].reshape(64, 1024),
            preferred_element_type=F32,
        )
        slots_out[pair] = value.astype(BF16).reshape(8, 16, 1024)
        here = picked.at[mine, pair]
        for way, device, rel in ((0, y_right, 0), (1, y_left, 1)):
            expert = far_y * 2 + (core if rel == 0 else 1 - core)
            rows_first.append(
                send(slots_out.at[pair, expert], rows_relay.at[way, pair],
                     rows_relay_sem, pair * 2 + way, device)
            )
        for way, to in ((0, right_y), (1, left_y)):
            for rel, device in ((0, at.at_y(to)), (1, at.across_y(to))):
                expert = to * 2 + (core if rel == 0 else 1 - core)
                near_rows.append(
                    send(slots_out.at[pair, expert], here, y_sem, pair * 4 + way * 2 + rel, device)
                )
        twin_rows.append(send(slots_out.at[pair, y * 2 + 1 - core], here, twin_sem, pair, twin))
        own_rows.append(move(slots_out.at[pair, mine], here, 13 + pair))

    def pass_rows(pair):
        for way, device, source in (
            (0, at.at_y(right_y), left_y), (1, at.across_y(left_y), right_y)
        ):
            rows_first[pair * 2 + way].wait_recv()
            rows_onward.append(
                send(rows_relay.at[way, pair], picked.at[source * 2 + core, pair],
                     rows_relay_sem, 8 + pair * 2 + way, device)
            )

    def spread_rows(messages, first, count):
        tile = one_hot(iota((128, count), 0) == first + iota((128, count), 1) % 32)
        return jnp.dot(messages, tile, preferred_element_type=F32).astype(BF16)

    next_rows(1)
    next_rows(2)
    arrive(by_z, [moved_z])
    moved_y = move(message_z.at[:, y], message_y.at[:, y], 6)
    by_y = [
        send(message_z.at[:, (y + step) % 4], message_y.at[:, y],
             message_sem, 7 + step, at.at_y(y + step))
        for step in (1, 2, 3)
    ]

    passed = jnp.concatenate(
        [message_z[block].reshape(8, 2, 128)[:, 0, :] for block in blocks], axis=0
    ).astype(BF16)
    slots, source = iota((512, 64), 0), iota((512, 64), 1)
    expand = one_hot(
        source == ((slots // 128) * 2 + (slots // 8) % 2) * 8 + (slots // 16) % 8
    )
    code = jnp.dot(expand, spread_rows(passed, 64, 64), preferred_element_type=F32)
    match = (
        (code == (slots % 2 + 1).astype(F32))
        & (source // 32 == (slots // 8) % 2)
        & ((source // 8) % 4 == (slots // 2) % 4)
    )
    pick[...] = one_hot(match).reshape(4, 128, 64)

    arrive([], moved_rows)
    send_rows(0)
    next_rows(3)
    send_rows(1)
    next_rows(4)
    next_rows(5)
    arrive(by_y, [moved_y])
    moved_core = move(message_y.at[:, :, core], message_all.at[tensor, :, :, core], 7)
    by_core = send(message_y.at[:, :, 1 - core], message_all.at[tensor, :, :, core],
                   message_sem, 0, twin)
    send_rows(2)
    pass_rows(0)
    next_rows(6)
    next_rows(7)
    arrive([by_core], [moved_core])
    here = message_all.at[tensor]
    across = send(here, here, spread_sem, 0, at.other_half())
    spread = [send(here, here, spread_sem, step, at.at_x(x + step)) for step in (1, 2, 3)]
    send_rows(3)
    pass_rows(1)
    pass_weight(0, up_first, up_direct)
    pass_rows(2)
    across.wait_recv()
    here = message_all.at[(1 - at.z_hi) * 4 + x]
    spread += [send(here, here, spread_sem, 3 + step, at.at_x(x + step)) for step in (1, 2, 3)]
    down_first, down_direct = send_weight(1)
    pass_rows(3)

    codes, gates = spread_rows(passed, 64, 256), spread_rows(passed, 96, 256)

    @pl.loop(0, 8)
    def _(expert):
        slots, source = iota((64, 64), 0), iota((64, 64), 1)
        expand = one_hot(source == (slots // 8) * 8 + expert)
        code = jnp.dot(expand, codes, preferred_element_type=F32)
        gate = jnp.dot(expand, gates, preferred_element_type=F32)
        slots, places = iota((64, 256), 0), iota((64, 256), 1)
        match = (
            (code == (slots % 2 + 1).astype(F32))
            & (places // 32 == slots // 8)
            & ((places // 8) % 4 == (slots // 2) % 4)
        )
        combine[expert] = jnp.where(match, gate, 0.0).astype(BF16)

    for rr in range(2):
        for c in range(3):
            for b in range(4):
                k, n = iota((128, 128), 0), iota((128, 128), 1)
                here = (k // 2 + b * 48 == c * 64 + n % 64) & (k % 2 == rr) & (k < 96)
                order_map[b * 128 : b * 128 + 128, (rr * 3 + c) * 128 : (rr * 3 + c) * 128 + 128] = (
                    one_hot(here)
                )
    arrive(spread)

    for t in range(8):
        right_rows[t] = message_all[t].reshape(64, 2, 128)[:, 1, :]
        entries[t * 16 : t * 16 + 16] = jnp.concatenate(
            [right_rows[t, pl.ds(b, 16, stride=4), :] for b in range(4)], axis=1
        ).astype(BF16)
    placed = jnp.dot(entries[...], order_map[...], preferred_element_type=F32)
    for t in range(8):
        for rr in range(2):
            for c in range(3):
                lanes = slice((rr * 3 + c) * 128, (rr * 3 + c) * 128 + 128)
                right_all[t * 2 + rr, pl.ds(c, 16, stride=3), :] = (
                    placed[t * 16 : t * 16 + 16, lanes]
                )

    arrive(up_direct[:4] + up_direct[6:], up_direct[4:6])

    widen = jnp.where(iota((8, 512), 1) // 64 == iota((8, 512), 0), 1.0, 0.0)

    @pl.loop(0, 8)
    def _(index):
        group, half = index // 2, index % 2
        left = message_all[at.z_hi * 4 + group, half * 4 + x].reshape(8, 2, 128)[:, 0, :]
        left_all[...] = contract_first(left, widen)
        for j in range(4):
            for lane in range(4):
                lanes = slice(lane * 128, lane * 128 + 128)
                delta = jnp.zeros((48, 128), F32)
                for r in range(16):
                    delta = delta + right_all[r] * left_all[r * 4 + j : r * 4 + j + 1, lanes]
                units = slice(j * 48, j * 48 + 48)
                weight[group, half, units, lanes] = (
                    up_all[half, group, units, lanes].astype(F32) + delta
                ).astype(BF16)

    pass_weight(1, down_first, down_direct)
    arrive(near_rows + twin_rows + rows_onward, own_rows)

    def project(group):
        total = jnp.zeros((192, 512), F32)
        for half in (0, 1):
            total = total + lax.dot_general(
                weight[group, half], picked[:, :, :, half * 512 : half * 512 + 512].reshape(512, 512),
                (((1,), (1,)), ((), ())), preferred_element_type=F32,
            )
        part[group] = total.astype(BF16)

    right_x, left_x, far_x = (x + 1) % 4, (x + 3) % 4, (x + 2) % 4
    top, low = pl.ds(0, 96), pl.ds(96, 96)
    project(far_x)
    copies = [
        send(part.at[far_x, top], hidden_far.at[0], hidden_sem, 0, x_right),
        send(part.at[far_x, low], hidden_far.at[1], hidden_sem, 1, x_left),
    ]
    project(right_x)
    copies.append(send(part.at[right_x, low], hidden_near.at[0, low], hidden_sem, 2, x_right))
    project(left_x)
    copies.append(send(part.at[left_x, top], hidden_near.at[1, top], hidden_sem, 3, x_left))
    copies[0].wait_recv()
    hidden_pass[0] = (part[right_x, top].astype(F32) + hidden_far[0].astype(F32)).astype(BF16)
    copies.append(send(hidden_pass.at[0], hidden_near.at[0, top], hidden_sem, 4, x_right))
    copies[1].wait_recv()
    hidden_pass[1] = (part[left_x, low].astype(F32) + hidden_far[1].astype(F32)).astype(BF16)
    copies.append(send(hidden_pass.at[1], hidden_near.at[1, low], hidden_sem, 5, x_left))
    project(x)
    arrive(copies[2:])
    value = part[x].astype(F32) + hidden_near[0].astype(F32) + hidden_near[1].astype(F32)
    hidden[x] = (value / (1.0 + jnp.exp(-value))).astype(BF16)
    here = hidden.at[x]
    from_left = send(here, here, gather_sem, 0, x_right)
    from_right = send(here, here, gather_sem, 1, x_left)
    from_left.wait_recv()
    here = hidden.at[left_x, top]
    far_top = send(here, here, gather_sem, 2, x_right)
    from_right.wait_recv()
    here = hidden.at[right_x, low]
    far_low = send(here, here, gather_sem, 3, x_left)
    arrive(down_direct[:4] + down_direct[6:], down_direct[4:6])
    arrive([far_top, far_low])

    twins, direct, relayed, own_slots = [], [], [], []
    for half in (0, 1):
        result[half] = (
            contract_first(hidden[...].reshape(768, 512), down_all[half].reshape(768, 512))
            .astype(BF16)
            .reshape(4, 2, 64, 512)
        )
        twins.append(send(result.at[half, :, 1 - core], twin_in.at[half], core_sem, half, twin))
        relayed.append(
            send(result.at[half, far_y, core], slots_relay.at[half, 0],
                 slots_relay_sem, half, y_right)
        )
        here = slots_in.at[half, y, core]
        direct.append(send(result.at[half, right_y, core], here, slots_sem, half * 2, y_right))
        direct.append(send(result.at[half, left_y, core], here, slots_sem, half * 2 + 1, y_left))
        own_slots.append(move(result.at[half, y, core], here, 8 + half))
    for half in (0, 1):
        twins[half].wait_recv()
        relayed.append(
            send(twin_in.at[half, far_y], slots_relay.at[half, 1],
                 slots_relay_sem, 2 + half, y_left)
        )
        here = slots_in.at[half, y, 1 - core]
        direct.append(send(twin_in.at[half, right_y], here, slots_sem, 4 + half * 2, y_right))
        direct.append(send(twin_in.at[half, left_y], here, slots_sem, 5 + half * 2, y_left))
        own_slots.append(move(twin_in.at[half, y], here, 10 + half))
    onward = []
    for half in (0, 1):
        relayed[half].wait_recv()
        onward.append(
            send(slots_relay.at[half, 0], slots_in.at[half, left_y, core],
                 slots_relay_sem, 4 + half, y_right)
        )
    for half in (0, 1):
        relayed[2 + half].wait_recv()
        onward.append(
            send(slots_relay.at[half, 1], slots_in.at[half, right_y, 1 - core],
                 slots_relay_sem, 6 + half, y_left)
        )
    for half in (0, 1):
        arrive(
            [direct[half * 2], direct[half * 2 + 1], direct[4 + half * 2], direct[5 + half * 2]]
            + [onward[half], onward[2 + half]],
            [own_slots[half], own_slots[2 + half]],
        )
        value = contract_first(
            combine[...].reshape(512, 256), slots_in[half].reshape(512, 512)
        )
        for group in range(8):
            line[half * 8 + blocks[group]] = value[group * 32 : group * 32 + 32]

    rights, lefts = [], []
    for step in range(8):
        value = line[(z + 8 - step) % 16]
        if step > 0:
            rights[step - 1].wait_recv()
            value = value + right_in[step - 1].astype(F32)
        right_out[step] = value.astype(BF16)
        rights.append(send(right_out.at[step], right_in.at[step], right_sem, step, z_right))
        if step < 7:
            value = line[(z + 9 + step) % 16]
            if step > 0:
                lefts[step - 1].wait_recv()
                value = value + left_in[step - 1].astype(F32)
            left_out[step] = value.astype(BF16)
            lefts.append(send(left_out.at[step], left_in.at[step], left_sem, step, z_left))
    lefts[6].wait_recv()
    rights[7].wait_recv()
    value = line[z] + right_in[7].astype(F32) + left_in[6].astype(F32)
    out[...] = value.astype(BF16)
    for copy in unsent:
        copy.wait_send()


def layer(up, down, rows, message):
    any_space = pl.BlockSpec(memory_space=pl.ANY)
    return pl.pallas_call(
        layer_kernel,
        out_shape=jax.ShapeDtypeStruct((32, 512), BF16),
        in_specs=[any_space] * 4,
        out_specs=pl.BlockSpec(memory_space=pltpu.VMEM),
        scratch_shapes=[
            pltpu.VMEM((2, 4, 192, 512), BF16),
            pltpu.VMEM((2, 4, 192, 512), BF16),
            pltpu.VMEM((2, 2, 192, 512), BF16),
            pltpu.VMEM((8, 32, 1024), BF16),
            pltpu.VMEM((4, 8, 16, 1024), BF16),
            pltpu.VMEM((2, 4, 16, 1024), BF16),
            pltpu.VMEM((8, 4, 2, 2, 128), F32),
            pltpu.VMEM((8, 4, 2, 2, 128), F32),
            pltpu.VMEM((8, 8, 4, 2, 2, 128), F32),
            pltpu.VMEM((4, 128, 64), BF16),
            pltpu.VMEM((8, 64, 256), BF16),
            pltpu.VMEM((512, 768), BF16),
            pltpu.VMEM((8, 64, 128), F32),
            pltpu.VMEM((128, 512), BF16),
            pltpu.VMEM((16, 48, 128), F32),
            pltpu.VMEM((128, 512), F32),
            pltpu.VMEM((4, 2, 192, 512), BF16),
            pltpu.VMEM((8, 4, 16, 1024), BF16),
            pltpu.VMEM((4, 192, 512), BF16),
            pltpu.VMEM((2, 96, 512), BF16),
            pltpu.VMEM((2, 192, 512), BF16),
            pltpu.VMEM((2, 96, 512), BF16),
            pltpu.VMEM((4, 192, 512), BF16),
            pltpu.VMEM((2, 4, 2, 64, 512), BF16),
            pltpu.VMEM((2, 4, 64, 512), BF16),
            pltpu.VMEM((2, 4, 2, 64, 512), BF16),
            pltpu.VMEM((2, 2, 64, 512), BF16),
            pltpu.VMEM((16, 32, 512), F32),
            pltpu.VMEM((8, 32, 512), BF16),
            pltpu.VMEM((7, 32, 512), BF16),
            pltpu.VMEM((8, 32, 512), BF16),
            pltpu.VMEM((7, 32, 512), BF16),
            pltpu.SemaphoreType.DMA((17,)),
            dma_sems(9),
            dma_sems(16),
            dma_sems(16),
            dma_sems(4),
            dma_sems(8),
            dma_sems(8),
            dma_sems(11),
            dma_sems(7),
            dma_sems(6),
            dma_sems(4),
            dma_sems(2),
            dma_sems(8),
            dma_sems(8),
            dma_sems(8),
            dma_sems(7),
        ],
        compiler_params=pltpu.CompilerParams(
            collective_id=0, has_side_effects=True, vmem_limit_bytes=VMEM_LIMIT
        ),
        name="layer",
    )(up, down, rows, message)


def body(
    core_left,
    core_right,
    grad_left,
    grad_right,
    first_left,
    first_right,
    second_left,
    second_right,
    up_base,
    down_base,
    states,
    routes,
    gates,
):
    cores = (
        core_left, core_right, grad_left, grad_right,
        first_left, first_right, second_left, second_right,
    )
    (
        left_next, right_next, first_left_next, first_right_next,
        second_left_next, second_right_next, message,
    ) = prepare(cores, routes.reshape(32, 8), gates.reshape(32, 8))
    mixed = layer(
        up_base[0], down_base[0], states.reshape(32, 4096), message.reshape(8, 4, 2, 2, 128)
    )
    mixed = mixed.reshape(4, 8, 512)
    return (
        mixed,
        left_next,
        right_next,
        first_left_next,
        first_right_next,
        second_left_next,
        second_right_next,
    )


def solution(mesh):
    cores = (P("tensor", "train"),) * 6
    in_specs = cores + (P("tensor", "train"),) * 2 + (
        P("train", "tensor", None),
        P("train", "tensor", None),
        P(None, "train", None),
        P(None, "train", None),
        P(None, "train", None),
    )
    out_specs = (P(None, "train", "tensor"),) + cores
    return jax.shard_map(body, mesh=mesh, in_specs=in_specs, out_specs=out_specs, check_vma=False)
```

```python
import jax
import jax.numpy as jnp
from jax import lax
from jax.experimental import pallas as pl
from jax.experimental.pallas import tpu as pltpu
from jax.sharding import PartitionSpec as P

MESH = pl.DeviceIdType.MESH
BF16 = jnp.bfloat16
F32 = jnp.float32

BETA_ONE = 0.9
BETA_TWO = 0.999
LEARN_RATE = 0.01
WEIGHT_DECAY = 0.1
EPSILON = 1e-08
STEP_NUMBER = 10.0

VMEM_LIMIT = 60 * 1024 * 1024


def adamw_update(value_now, gradient, first_moment, second_moment):
    first_next = BETA_ONE * first_moment + (1.0 - BETA_ONE) * gradient
    second_next = BETA_TWO * second_moment + (1.0 - BETA_TWO) * gradient * gradient
    first_scale = 1.0 - BETA_ONE**STEP_NUMBER
    second_scale = 1.0 - BETA_TWO**STEP_NUMBER
    update = first_next / first_scale / (jnp.sqrt(second_next / second_scale) + EPSILON)
    value_next = value_now - LEARN_RATE * (update + WEIGHT_DECAY * value_now)
    return (value_next, first_next, second_next)


def prepare_kernel(
    core_left, core_right, grad_left, grad_right, first_left, first_right, second_left, second_right,
    routes, gates,
    left_next, right_next, first_left_next, first_right_next, second_left_next, second_right_next,
    message, entries,
):
    left, first, second = adamw_update(
        core_left[...], grad_left[...], first_left[...], second_left[...]
    )
    left_next[...], first_left_next[...], second_left_next[...] = left, first, second
    right, first, second = adamw_update(
        core_right[...], grad_right[...], first_right[...], second_right[...]
    )
    right_next[...], first_right_next[...], second_right_next[...] = right, first, second

    for r in range(16):
        entries[0, r * 4 : r * 4 + 4] = left[:, r * 64 : r * 64 + 64]
    for pair in range(48):
        entries[1, pair * 2 : pair * 2 + 2] = right[:, pair * 64 : pair * 64 + 64]
    entries[1, 96:128] = jnp.zeros((32, 64), F32)
    expert = lax.broadcasted_iota(jnp.int32, (32, 64), 1)
    taken, weight = jnp.zeros((32, 64), F32), jnp.zeros((32, 64), F32)
    for k in range(8):
        chosen = routes[:, k : k + 1] == expert
        taken = taken + jnp.where(chosen, 1.0, 0.0)
        weight = weight + jnp.where(chosen, gates[:, k : k + 1], 0.0)
    to, by = (lax.broadcasted_iota(jnp.int32, (32, 32), dim) for dim in (0, 1))
    before = jnp.where((by < to) & (by // 8 == to // 8), 1.0, 0.0)
    earlier = jnp.dot(before, taken, preferred_element_type=F32)
    entries[0, 64:96] = taken * (earlier + 1.0)
    entries[0, 96:128] = weight
    row, column = (lax.broadcasted_iota(jnp.int32, (128, 128), dim) for dim in (0, 1))
    same = jnp.where(row == column, 1.0, 0.0).astype(BF16)
    for kind in range(2):
        message[kind] = lax.dot_general(
            entries[kind].astype(BF16), same, (((0,), (0,)), ((), ())), preferred_element_type=F32
        )


def prepare(cores, routes, gates):
    return pl.pallas_call(
        prepare_kernel,
        out_shape=(
            *(jax.ShapeDtypeStruct(shape, F32) for shape in ((4, 1024), (2, 3072)) * 3),
            jax.ShapeDtypeStruct((2, 64, 128), F32),
        ),
        scratch_shapes=[pltpu.VMEM((2, 128, 64), F32)],
        name="prepare",
    )(*cores, routes, gates)


class Place:
    def __init__(self):
        self.train = lax.axis_index("train")
        self.tensor = lax.axis_index("tensor")
        self.core = self.train % 2
        self.y = (self.train // 2) % 4
        self.z_lo = self.train // 8
        self.x = self.tensor % 4
        self.z_hi = self.tensor // 4
        self.z = self.z_hi * 8 + self.z_lo

    def at_z(self, z):
        z = (z + 16) % 16
        return ((z % 8) * 8 + self.y * 2 + self.core, (z // 8) * 4 + self.x)

    def at_y(self, y):
        return (self.z_lo * 8 + ((y + 4) % 4) * 2 + self.core, self.tensor)

    def at_x(self, x):
        return (self.train, self.z_hi * 4 + (x + 4) % 4)

    def across_y(self, y):
        return (self.z_lo * 8 + ((y + 4) % 4) * 2 + 1 - self.core, self.tensor)

    def twin(self):
        return (self.train + 1 - 2 * self.core, self.tensor)

    def other_half(self):
        return (self.train, (1 - self.z_hi) * 4 + self.x)


def push(src, dst, sems, index, device):
    copy = pltpu.make_async_remote_copy(
        src_ref=src,
        dst_ref=dst,
        send_sem=sems.at[0, index],
        recv_sem=sems.at[1, index],
        device_id=device,
        device_id_type=MESH,
    )
    copy.start()
    return copy


def signal(device):
    pl.semaphore_signal(
        pltpu.get_barrier_semaphore(), inc=1, device_id=device, device_id_type=MESH
    )


def dma_sems(count):
    return pltpu.SemaphoreType.DMA((2, count))


def iota(shape, dim):
    return lax.broadcasted_iota(jnp.int32, shape, dim)


def one_hot(condition):
    return jnp.where(condition, 1.0, 0.0).astype(BF16)


def contract_first(left, right):
    return lax.dot_general(left, right, (((0,), (0,)), ((), ())), preferred_element_type=F32)


def layer_kernel(
    up, down, rows, message, out,
    up_all, down_all, relay, rows_z, slots_out, rows_relay, message_z, message_y, message_all,
    pick, combine, order_map, right_rows, entries, right_all, left_all, weight, picked,
    part, hidden_far, hidden_near, hidden_pass, hidden,
    result, twin_in, slots_in, slots_relay, line, right_in, left_in, right_out, left_out,
    local_sem, z_sem, y_sem, rows_relay_sem, twin_sem, weight_sem, relay_sem,
    message_sem, spread_sem, hidden_sem, gather_sem,
    core_sem, slots_sem, slots_relay_sem, right_sem, left_sem,
):
    at = Place()
    tensor, x, y, z_lo, z, core = at.tensor, at.x, at.y, at.z_lo, at.z, at.core
    twin = at.twin()
    x_right, x_left = at.at_x(x + 1), at.at_x(x - 1)
    y_right, y_left = at.at_y(y + 1), at.at_y(y - 1)
    z_right, z_left = at.at_z(z + 1), at.at_z(z - 1)

    def same_half(step):
        return (((z_lo + step) % 8) * 8 + y * 2 + core, tensor)

    for step in range(1, 8):
        signal(same_half(step))
    for step in (1, 2, 3):
        signal(at.at_x(x + step))
        signal(at.at_y(y + step))
    for device in (twin, z_right, z_left, at.other_half()):
        signal(device)
    signal(at.across_y(y + 1))
    signal(at.across_y(y - 1))
    pl.semaphore_wait(pltpu.get_barrier_semaphore(), 19)

    unsent = []

    def send(src, dst, sems, index, device):
        copy = push(src, dst, sems, index, device)
        unsent.append(copy)
        return copy

    def move(src, dst, index):
        copy = pltpu.make_async_copy(src, dst, local_sem.at[index])
        copy.start()
        return copy

    def columns_of(half, to):
        return pl.ds(pl.multiple_of((half * 4 + to) * 512, 512), 512)

    halves = [
        (rows.at[:, columns_of(half, x)], pl.ds(half * 512, 512)) for half in (0, 1)
    ]
    z_rights, z_lefts = [], []
    for half, (origin, lanes) in enumerate(halves):
        z_rights.append(send(origin, rows_z.at[1, :, lanes], z_sem, half, z_right))
        z_lefts.append(send(origin, rows_z.at[2, :, lanes], z_sem, 2 + half, z_left))
    moved_rows = [
        move(origin, rows_z.at[0, :, lanes], half * 11 + 1)
        for half, (origin, lanes) in enumerate(halves)
    ]

    moved_z = move(message.at[:, z_lo], message_z.at[:, z_lo], 0)
    by_z = [
        send(message.at[:, (z_lo + step) % 8], message_z.at[:, z_lo], message_sem, step, same_half(step))
        for step in range(1, 8)
    ]

    weights = ((up, up_all), (down, down_all))

    def first_weight(w):
        return [
            send(weights[w][0].at[:, columns_of(way, (x + 2) % 4)], relay.at[w, way],
                 relay_sem, w * 2 + way, device)
            for way, device in ((0, x_right), (1, x_left))
        ]

    def direct_weight(w):
        origin, dst = weights[w]
        direct = []
        for way, device, to in ((0, x_right, (x + 1) % 4), (1, x_left, (x + 3) % 4)):
            for half in (0, 1):
                direct.append(
                    send(origin.at[:, columns_of(half, to)], dst.at[half, x],
                         weight_sem, w * 4 + way * 2 + half, device)
                )
        for half in (0, 1):
            direct.append(move(origin.at[:, columns_of(half, x)], dst.at[half, x], 2 + w * 2 + half))
        return direct

    def pass_weight(w, first, direct):
        dst = weights[w][1]
        for way, device, source in ((0, x_right, (x + 3) % 4), (1, x_left, (x + 1) % 4)):
            first[way].wait_recv()
            direct.append(
                send(relay.at[w, way], dst.at[way, source], relay_sem, 4 + w * 2 + way, device)
            )

    def arrive(copies, own=()):
        for copy in copies:
            copy.wait_recv()
        for copy in own:
            copy.wait()

    up_first, up_direct = first_weight(0), direct_weight(0)

    blocks = [z_lo]
    for order in range(1, 8):
        step = (order + 1) // 2
        blocks.append((z_lo - step + 8) % 8 if order % 2 == 1 else (z_lo + step) % 8)

    def next_rows(order):
        if order == 1:
            arrive(z_rights[:2])
        elif order == 2:
            arrive(z_lefts[:2])
        elif order % 2 == 1:
            z_rights[order // 2 + 1].wait_recv()
        else:
            z_lefts[order // 2].wait_recv()
        here = rows_z.at[order]
        if order in (1, 3, 5):
            z_rights.append(send(here, rows_z.at[order + 2], z_sem, 3 + order, z_right))
        elif order in (2, 4):
            z_lefts.append(send(here, rows_z.at[order + 2], z_sem, 3 + order, z_left))

    right_y, left_y, far_y = (y + 1) % 4, (y + 3) % 4, (y + 2) % 4
    near_rows, twin_rows, rows_first, rows_onward, own_rows = [], [], [], [], []
    mine = y * 2 + core

    def send_rows(pair):
        value = jnp.dot(
            pick[pair],
            rows_z[pair * 2 : pair * 2 + 2].reshape(64, 1024),
            preferred_element_type=F32,
        )
        slots_out[pair] = value.astype(BF16).reshape(8, 16, 1024)
        here = picked.at[mine, pair]
        for way, device, rel in ((0, y_right, 0), (1, y_left, 1)):
            expert = far_y * 2 + (core if rel == 0 else 1 - core)
            rows_first.append(
                send(slots_out.at[pair, expert], rows_relay.at[way, pair],
                     rows_relay_sem, pair * 2 + way, device)
            )
        for way, to in ((0, right_y), (1, left_y)):
            for rel, device in ((0, at.at_y(to)), (1, at.across_y(to))):
                expert = to * 2 + (core if rel == 0 else 1 - core)
                near_rows.append(
                    send(slots_out.at[pair, expert], here, y_sem, pair * 4 + way * 2 + rel, device)
                )
        twin_rows.append(send(slots_out.at[pair, y * 2 + 1 - core], here, twin_sem, pair, twin))
        own_rows.append(move(slots_out.at[pair, mine], here, 13 + pair))

    def pass_rows(pair):
        for way, device, source in (
            (0, at.at_y(right_y), left_y), (1, at.across_y(left_y), right_y)
        ):
            rows_first[pair * 2 + way].wait_recv()
            rows_onward.append(
                send(rows_relay.at[way, pair], picked.at[source * 2 + core, pair],
                     rows_relay_sem, 8 + pair * 2 + way, device)
            )

    def spread_rows(messages, first, count):
        tile = one_hot(iota((128, count), 0) == first + iota((128, count), 1) % 32)
        return jnp.dot(messages, tile, preferred_element_type=F32).astype(BF16)

    next_rows(1)
    next_rows(2)
    arrive(by_z, [moved_z])
    moved_y = move(message_z.at[:, :, y], message_y.at[:, :, y], 6)
    by_y = [
        send(message_z.at[:, :, (y + step) % 4], message_y.at[:, :, y],
             message_sem, 7 + step, at.at_y(y + step))
        for step in (1, 2, 3)
    ]

    passed = jnp.concatenate(
        [message_z[0, block].reshape(8, 128) for block in blocks], axis=0
    ).astype(BF16)
    slots, source = iota((512, 64), 0), iota((512, 64), 1)
    expand = one_hot(
        source == ((slots // 128) * 2 + (slots // 8) % 2) * 8 + (slots // 16) % 8
    )
    code = jnp.dot(expand, spread_rows(passed, 64, 64), preferred_element_type=F32)
    match = (
        (code == (slots % 2 + 1).astype(F32))
        & (source // 32 == (slots // 8) % 2)
        & ((source // 8) % 4 == (slots // 2) % 4)
    )
    pick[...] = one_hot(match).reshape(4, 128, 64)

    arrive(by_y, [moved_y])
    here = message_all.at[tensor, :, :, :, core]
    moved_core = move(message_y.at[:, :, :, core], here, 7)
    by_core = send(message_y.at[:, :, :, 1 - core], here, message_sem, 0, twin)
    next_rows(3)
    arrive([], moved_rows)
    send_rows(0)
    arrive([by_core], [moved_core])
    here = message_all.at[tensor, 1]
    across = send(here, here, spread_sem, 0, at.other_half())
    here = message_all.at[tensor]
    spread = [send(here, here, spread_sem, step, at.at_x(x + step)) for step in (1, 2, 3)]
    next_rows(4)
    send_rows(1)
    next_rows(5)
    pass_weight(0, up_first, up_direct)
    down_first = first_weight(1)
    send_rows(2)
    pass_rows(0)
    next_rows(6)
    next_rows(7)
    send_rows(3)
    pass_rows(1)
    across.wait_recv()
    here = message_all.at[(1 - at.z_hi) * 4 + x, 1]
    spread += [send(here, here, spread_sem, 3 + step, at.at_x(x + step)) for step in (1, 2, 3)]
    down_direct = direct_weight(1)
    pass_rows(2)
    pass_rows(3)

    codes, gates = spread_rows(passed, 64, 256), spread_rows(passed, 96, 256)

    @pl.loop(0, 8)
    def _(expert):
        slots, source = iota((64, 64), 0), iota((64, 64), 1)
        expand = one_hot(source == (slots // 8) * 8 + expert)
        code = jnp.dot(expand, codes, preferred_element_type=F32)
        gate = jnp.dot(expand, gates, preferred_element_type=F32)
        slots, places = iota((64, 256), 0), iota((64, 256), 1)
        match = (
            (code == (slots % 2 + 1).astype(F32))
            & (places // 32 == slots // 8)
            & ((places // 8) % 4 == (slots // 2) % 4)
        )
        value = jnp.where(match, gate, 0.0).astype(BF16)
        for part_at in (0, 1):
            combine[part_at, expert] = value[
                part_at * 32 : part_at * 32 + 32, part_at * 128 : part_at * 128 + 128
            ]

    for rr in range(2):
        for c in range(3):
            for b in range(4):
                k, n = iota((128, 128), 0), iota((128, 128), 1)
                here = (k // 2 + b * 48 == c * 64 + n % 64) & (k % 2 == rr) & (k < 96)
                order_map[b * 128 : b * 128 + 128, (rr * 3 + c) * 128 : (rr * 3 + c) * 128 + 128] = (
                    one_hot(here)
                )
    arrive(spread)

    for t in range(8):
        right_rows[t] = message_all[t, 1].reshape(64, 128)
        entries[t * 16 : t * 16 + 16] = jnp.concatenate(
            [right_rows[t, pl.ds(b, 16, stride=4), :] for b in range(4)], axis=1
        ).astype(BF16)
    placed = jnp.dot(entries[...], order_map[...], preferred_element_type=F32)
    for t in range(8):
        for rr in range(2):
            for c in range(3):
                lanes = slice((rr * 3 + c) * 128, (rr * 3 + c) * 128 + 128)
                right_all[t * 2 + rr, pl.ds(c, 16, stride=3), :] = (
                    placed[t * 16 : t * 16 + 16, lanes]
                )

    arrive(up_direct[:4] + up_direct[6:], up_direct[4:6])

    widen = jnp.where(iota((8, 512), 1) // 64 == iota((8, 512), 0), 1.0, 0.0)

    def weigh(group):
        @pl.loop(0, 2)
        def _(half):
            left = message_all[at.z_hi * 4 + group, 0, half * 4 + x].reshape(8, 128)
            left_all[...] = contract_first(left, widen)
            for j in range(4):
                for lane in range(4):
                    lanes = slice(lane * 128, lane * 128 + 128)
                    delta = jnp.zeros((48, 128), F32)
                    for r in range(16):
                        delta = delta + right_all[r] * left_all[r * 4 + j : r * 4 + j + 1, lanes]
                    units = slice(j * 48, j * 48 + 48)
                    weight[group, half, units, lanes] = (
                        up_all[half, group, units, lanes].astype(F32) + delta
                    ).astype(BF16)

    def project(group, ab):
        total = jnp.zeros((192, 256), F32)
        for half in (0, 1):
            here = picked[:, ab * 2 : ab * 2 + 2, :, half * 512 : half * 512 + 512]
            total = total + lax.dot_general(
                weight[group, half], here.reshape(256, 512),
                (((1,), (1,)), ((), ())), preferred_element_type=F32,
            )
        part[ab, group] = total.astype(BF16)

    both = (0, 1)
    right_x, left_x, far_x = (x + 1) % 4, (x + 3) % 4, (x + 2) % 4
    top, low = pl.ds(0, 96), pl.ds(96, 96)
    far_parts, near_parts = [], [[], []]
    weigh(far_x)
    for ab in both:
        arrive(
            near_rows[ab * 8 : ab * 8 + 8] + twin_rows[ab * 2 : ab * 2 + 2]
            + rows_onward[ab * 4 : ab * 4 + 4],
            own_rows[ab * 2 : ab * 2 + 2],
        )
        project(far_x, ab)
        far_parts.append([
            send(part.at[ab, far_x, top], hidden_far.at[ab, 0], hidden_sem, ab * 6, x_right),
            send(part.at[ab, far_x, low], hidden_far.at[ab, 1], hidden_sem, ab * 6 + 1, x_left),
        ])
    weigh(right_x)
    for ab in both:
        project(right_x, ab)
        near_parts[ab].append(
            send(part.at[ab, right_x, low], hidden_near.at[ab, 0, low], hidden_sem, ab * 6 + 2, x_right)
        )
    weigh(left_x)
    for ab in both:
        project(left_x, ab)
        near_parts[ab].append(
            send(part.at[ab, left_x, top], hidden_near.at[ab, 1, top], hidden_sem, ab * 6 + 3, x_left)
        )
    for ab in both:
        for way, device, to, units in ((0, x_right, right_x, top), (1, x_left, left_x, low)):
            far_parts[ab][way].wait_recv()
            hidden_pass[ab, way] = (
                part[ab, to, units].astype(F32) + hidden_far[ab, way].astype(F32)
            ).astype(BF16)
            near_parts[ab].append(
                send(hidden_pass.at[ab, way], hidden_near.at[ab, way, units],
                     hidden_sem, ab * 6 + 4 + way, device)
            )
    pass_weight(1, down_first, down_direct)
    weigh(x)
    for ab in both:
        project(x, ab)
    gathers = []
    for ab in both:
        arrive(near_parts[ab])
        value = (
            part[ab, x].astype(F32)
            + hidden_near[ab, 0].astype(F32) + hidden_near[ab, 1].astype(F32)
        )
        hidden[ab, x] = (value / (1.0 + jnp.exp(-value))).astype(BF16)
        here = hidden.at[ab, x]
        gathers.append([
            send(here, here, gather_sem, ab * 4, x_right),
            send(here, here, gather_sem, ab * 4 + 1, x_left),
        ])
    for ab in both:
        for way, device, source, units in ((0, x_right, left_x, top), (1, x_left, right_x, low)):
            gathers[ab][way].wait_recv()
            here = hidden.at[ab, source, units]
            gathers[ab].append(send(here, here, gather_sem, ab * 4 + 2 + way, device))
    arrive(down_direct[:4] + down_direct[6:], down_direct[4:6])

    twins, relayed, direct, onward = [], [[], []], [[], []], [[], []]
    own_slots = [[], []]
    for ab in both:
        arrive(gathers[ab][2:])
        for half in (0, 1):
            value = contract_first(
                hidden[ab].reshape(768, 256), down_all[half].reshape(768, 512)
            )
            result[ab, :, :, :, half * 512 : half * 512 + 512] = (
                value.astype(BF16).reshape(4, 2, 32, 512)
            )
        twins.append(send(result.at[ab, :, 1 - core], twin_in.at[ab], core_sem, ab, twin))
        relayed[ab].append(
            send(result.at[ab, far_y, core], slots_relay.at[ab, 0], slots_relay_sem, ab, y_right)
        )
        here = slots_in.at[ab, y, core]
        direct[ab].append(send(result.at[ab, right_y, core], here, slots_sem, ab * 2, y_right))
        direct[ab].append(send(result.at[ab, left_y, core], here, slots_sem, ab * 2 + 1, y_left))
        own_slots[ab].append(move(result.at[ab, y, core], here, 8 + ab))

    def pass_twin(ab):
        twins[ab].wait_recv()
        relayed[ab].append(
            send(twin_in.at[ab, far_y], slots_relay.at[ab, 1], slots_relay_sem, 2 + ab, y_left)
        )
        here = slots_in.at[ab, y, 1 - core]
        direct[ab].append(send(twin_in.at[ab, right_y], here, slots_sem, 4 + ab * 2, y_right))
        direct[ab].append(send(twin_in.at[ab, left_y], here, slots_sem, 5 + ab * 2, y_left))
        own_slots[ab].append(move(twin_in.at[ab, y], here, 10 + ab))

    def pass_slots(ab, way):
        device, source, from_core = ((y_right, left_y, core), (y_left, right_y, 1 - core))[way]
        relayed[ab][way].wait_recv()
        onward[ab].append(
            send(slots_relay.at[ab, way], slots_in.at[ab, source, from_core],
                 slots_relay_sem, 4 + way * 2 + ab, device)
        )

    def mix_slots(ab):
        arrive(direct[ab] + onward[ab], own_slots[ab])
        value = contract_first(
            combine[ab].reshape(256, 128), slots_in[ab].reshape(256, 1024)
        )
        for order in range(4):
            for half in (0, 1):
                line[half * 8 + blocks[ab * 4 + order]] = (
                    value[order * 32 : order * 32 + 32, half * 512 : half * 512 + 512]
                )

    pass_twin(0)
    pass_slots(0, 0)
    pass_twin(1)
    pass_slots(0, 1)
    pass_slots(1, 0)
    mix_slots(0)
    pass_slots(1, 1)
    mix_slots(1)

    rights, lefts = [], []
    pieces = (slice(0, 16), slice(16, 32))
    for step in range(8):
        for piece, rows_at in enumerate(pieces):
            value = line[(z + 8 - step) % 16, rows_at]
            if step > 0:
                rights[step * 2 - 2 + piece].wait_recv()
                value = value + right_in[step - 1, rows_at].astype(F32)
            right_out[step, rows_at] = value.astype(BF16)
            there = pl.ds(piece * 16, 16)
            rights.append(
                send(right_out.at[step, there], right_in.at[step, there],
                     right_sem, step * 2 + piece, z_right)
            )
            if step < 7:
                value = line[(z + 9 + step) % 16, rows_at]
                if step > 0:
                    lefts[step * 2 - 2 + piece].wait_recv()
                    value = value + left_in[step - 1, rows_at].astype(F32)
                left_out[step, rows_at] = value.astype(BF16)
                lefts.append(
                    send(left_out.at[step, there], left_in.at[step, there],
                         left_sem, step * 2 + piece, z_left)
                )
    for piece, rows_at in enumerate(pieces):
        lefts[12 + piece].wait_recv()
        rights[14 + piece].wait_recv()
        value = line[z, rows_at] + right_in[7, rows_at].astype(F32) + left_in[6, rows_at].astype(F32)
        out[rows_at, :] = value.astype(BF16)
    for copy in unsent:
        copy.wait_send()


def layer(up, down, rows, message):
    any_space = pl.BlockSpec(memory_space=pl.ANY)
    return pl.pallas_call(
        layer_kernel,
        out_shape=jax.ShapeDtypeStruct((32, 512), BF16),
        in_specs=[any_space] * 4,
        out_specs=pl.BlockSpec(memory_space=pltpu.VMEM),
        scratch_shapes=[
            pltpu.VMEM((2, 4, 192, 512), BF16),
            pltpu.VMEM((2, 4, 192, 512), BF16),
            pltpu.VMEM((2, 2, 192, 512), BF16),
            pltpu.VMEM((8, 32, 1024), BF16),
            pltpu.VMEM((4, 8, 16, 1024), BF16),
            pltpu.VMEM((2, 4, 16, 1024), BF16),
            pltpu.VMEM((2, 8, 4, 2, 1, 128), F32),
            pltpu.VMEM((2, 8, 4, 2, 1, 128), F32),
            pltpu.VMEM((8, 2, 8, 4, 2, 1, 128), F32),
            pltpu.VMEM((4, 128, 64), BF16),
            pltpu.VMEM((2, 8, 32, 128), BF16),
            pltpu.VMEM((512, 768), BF16),
            pltpu.VMEM((8, 64, 128), F32),
            pltpu.VMEM((128, 512), BF16),
            pltpu.VMEM((16, 48, 128), F32),
            pltpu.VMEM((128, 512), F32),
            pltpu.VMEM((4, 2, 192, 512), BF16),
            pltpu.VMEM((8, 4, 16, 1024), BF16),
            pltpu.VMEM((2, 4, 192, 256), BF16),
            pltpu.VMEM((2, 2, 96, 256), BF16),
            pltpu.VMEM((2, 2, 192, 256), BF16),
            pltpu.VMEM((2, 2, 96, 256), BF16),
            pltpu.VMEM((2, 4, 192, 256), BF16),
            pltpu.VMEM((2, 4, 2, 32, 1024), BF16),
            pltpu.VMEM((2, 4, 32, 1024), BF16),
            pltpu.VMEM((2, 4, 2, 32, 1024), BF16),
            pltpu.VMEM((2, 2, 32, 1024), BF16),
            pltpu.VMEM((16, 32, 512), F32),
            pltpu.VMEM((8, 32, 512), BF16),
            pltpu.VMEM((7, 32, 512), BF16),
            pltpu.VMEM((8, 32, 512), BF16),
            pltpu.VMEM((7, 32, 512), BF16),
            pltpu.SemaphoreType.DMA((17,)),
            dma_sems(9),
            dma_sems(16),
            dma_sems(16),
            dma_sems(4),
            dma_sems(8),
            dma_sems(8),
            dma_sems(11),
            dma_sems(7),
            dma_sems(12),
            dma_sems(8),
            dma_sems(2),
            dma_sems(8),
            dma_sems(8),
            dma_sems(16),
            dma_sems(14),
        ],
        compiler_params=pltpu.CompilerParams(
            collective_id=0, has_side_effects=True, vmem_limit_bytes=VMEM_LIMIT
        ),
        name="layer",
    )(up, down, rows, message)


def body(
    core_left,
    core_right,
    grad_left,
    grad_right,
    first_left,
    first_right,
    second_left,
    second_right,
    up_base,
    down_base,
    states,
    routes,
    gates,
):
    cores = (
        core_left, core_right, grad_left, grad_right,
        first_left, first_right, second_left, second_right,
    )
    (
        left_next, right_next, first_left_next, first_right_next,
        second_left_next, second_right_next, message,
    ) = prepare(cores, routes.reshape(32, 8), gates.reshape(32, 8))
    mixed = layer(
        up_base[0], down_base[0], states.reshape(32, 4096), message.reshape(2, 8, 4, 2, 1, 128)
    )
    mixed = mixed.reshape(4, 8, 512)
    return (
        mixed,
        left_next,
        right_next,
        first_left_next,
        first_right_next,
        second_left_next,
        second_right_next,
    )


def solution(mesh):
    cores = (P("tensor", "train"),) * 6
    in_specs = cores + (P("tensor", "train"),) * 2 + (
        P("train", "tensor", None),
        P("train", "tensor", None),
        P(None, "train", None),
        P(None, "train", None),
        P(None, "train", None),
    )
    out_specs = (P(None, "train", "tensor"),) + cores
    return jax.shard_map(body, mesh=mesh, in_specs=in_specs, out_specs=out_specs, check_vma=False)
```

```python
import jax
import jax.numpy as jnp
from jax import lax
from jax.experimental import pallas as pl
from jax.experimental.pallas import tpu as pltpu
from jax.sharding import PartitionSpec as P

MESH = pl.DeviceIdType.MESH
BF16 = jnp.bfloat16
F32 = jnp.float32

BETA_ONE = 0.9
BETA_TWO = 0.999
LEARN_RATE = 0.01
WEIGHT_DECAY = 0.1
EPSILON = 1e-08
STEP_NUMBER = 10.0

VMEM_LIMIT = 60 * 1024 * 1024


def adamw_update(value_now, gradient, first_moment, second_moment):
    first_next = BETA_ONE * first_moment + (1.0 - BETA_ONE) * gradient
    second_next = BETA_TWO * second_moment + (1.0 - BETA_TWO) * gradient * gradient
    first_scale = 1.0 - BETA_ONE**STEP_NUMBER
    second_scale = 1.0 - BETA_TWO**STEP_NUMBER
    update = first_next / first_scale / (jnp.sqrt(second_next / second_scale) + EPSILON)
    value_next = value_now - LEARN_RATE * (update + WEIGHT_DECAY * value_now)
    return (value_next, first_next, second_next)


def prepare_kernel(
    core_left, core_right, grad_left, grad_right, first_left, first_right, second_left, second_right,
    routes, gates,
    left_next, right_next, first_left_next, first_right_next, second_left_next, second_right_next,
    message, entries,
):
    left, first, second = adamw_update(
        core_left[...], grad_left[...], first_left[...], second_left[...]
    )
    left_next[...], first_left_next[...], second_left_next[...] = left, first, second
    right, first, second = adamw_update(
        core_right[...], grad_right[...], first_right[...], second_right[...]
    )
    right_next[...], first_right_next[...], second_right_next[...] = right, first, second

    for r in range(16):
        entries[0, r * 4 : r * 4 + 4] = left[:, r * 64 : r * 64 + 64]
    for pair in range(48):
        entries[1, pair * 2 : pair * 2 + 2] = right[:, pair * 64 : pair * 64 + 64]
    entries[1, 96:128] = jnp.zeros((32, 64), F32)
    expert = lax.broadcasted_iota(jnp.int32, (32, 64), 1)
    taken, weight = jnp.zeros((32, 64), F32), jnp.zeros((32, 64), F32)
    for k in range(8):
        chosen = routes[:, k : k + 1] == expert
        taken = taken + jnp.where(chosen, 1.0, 0.0)
        weight = weight + jnp.where(chosen, gates[:, k : k + 1], 0.0)
    to, by = (lax.broadcasted_iota(jnp.int32, (32, 32), dim) for dim in (0, 1))
    before = jnp.where((by < to) & (by // 8 == to // 8), 1.0, 0.0)
    earlier = jnp.dot(before, taken, preferred_element_type=F32)
    entries[0, 64:96] = taken * (earlier + 1.0)
    entries[0, 96:128] = weight
    row, column = (lax.broadcasted_iota(jnp.int32, (128, 128), dim) for dim in (0, 1))
    same = jnp.where(row == column, 1.0, 0.0).astype(BF16)
    for kind in range(2):
        message[kind] = lax.dot_general(
            entries[kind].astype(BF16), same, (((0,), (0,)), ((), ())), preferred_element_type=F32
        )


def prepare(cores, routes, gates):
    return pl.pallas_call(
        prepare_kernel,
        out_shape=(
            *(jax.ShapeDtypeStruct(shape, F32) for shape in ((4, 1024), (2, 3072)) * 3),
            jax.ShapeDtypeStruct((2, 64, 128), F32),
        ),
        scratch_shapes=[pltpu.VMEM((2, 128, 64), F32)],
        name="prepare",
    )(*cores, routes, gates)


class Place:
    def __init__(self):
        self.train = lax.axis_index("train")
        self.tensor = lax.axis_index("tensor")
        self.core = self.train % 2
        self.y = (self.train // 2) % 4
        self.z_lo = self.train // 8
        self.x = self.tensor % 4
        self.z_hi = self.tensor // 4
        self.z = self.z_hi * 8 + self.z_lo

    def at_z(self, z):
        z = (z + 16) % 16
        return ((z % 8) * 8 + self.y * 2 + self.core, (z // 8) * 4 + self.x)

    def at_y(self, y):
        return (self.z_lo * 8 + ((y + 4) % 4) * 2 + self.core, self.tensor)

    def at_x(self, x):
        return (self.train, self.z_hi * 4 + (x + 4) % 4)

    def across_y(self, y):
        return (self.z_lo * 8 + ((y + 4) % 4) * 2 + 1 - self.core, self.tensor)

    def twin(self):
        return (self.train + 1 - 2 * self.core, self.tensor)

    def other_half(self):
        return (self.train, (1 - self.z_hi) * 4 + self.x)


def push(src, dst, sems, index, device):
    copy = pltpu.make_async_remote_copy(
        src_ref=src,
        dst_ref=dst,
        send_sem=sems.at[0, index],
        recv_sem=sems.at[1, index],
        device_id=device,
        device_id_type=MESH,
    )
    copy.start()
    return copy


def signal(device):
    pl.semaphore_signal(
        pltpu.get_barrier_semaphore(), inc=1, device_id=device, device_id_type=MESH
    )


def dma_sems(count):
    return pltpu.SemaphoreType.DMA((2, count))


def iota(shape, dim):
    return lax.broadcasted_iota(jnp.int32, shape, dim)


def one_hot(condition):
    return jnp.where(condition, 1.0, 0.0).astype(BF16)


def contract_first(left, right):
    return lax.dot_general(left, right, (((0,), (0,)), ((), ())), preferred_element_type=F32)


def layer_kernel(
    up, down, rows, message, out,
    up_all, down_all, relay, rows_z, slots_out, rows_relay, message_z, message_y, message_own, left_in_x,
    pick, combine, order_map, right_rows, entries, right_all, left_all, weight, picked,
    part, hidden_far, hidden_near, hidden_pass, hidden,
    result, twin_in, slots_in, slots_relay, line, right_in, left_in, right_out, left_out,
    local_sem, z_sem, y_sem, rows_relay_sem, twin_sem, weight_sem, relay_sem,
    message_sem, spread_sem, hidden_sem, gather_sem,
    core_sem, slots_sem, slots_relay_sem, right_sem, left_sem,
):
    at = Place()
    tensor, x, y, z_lo, z, core = at.tensor, at.x, at.y, at.z_lo, at.z, at.core
    twin = at.twin()
    x_right, x_left = at.at_x(x + 1), at.at_x(x - 1)
    y_right, y_left = at.at_y(y + 1), at.at_y(y - 1)
    z_right, z_left = at.at_z(z + 1), at.at_z(z - 1)

    def same_half(step):
        return (((z_lo + step) % 8) * 8 + y * 2 + core, tensor)

    for step in range(1, 8):
        signal(same_half(step))
    for step in (1, 2, 3):
        signal(at.at_x(x + step))
        signal(at.at_y(y + step))
    for device in (twin, z_right, z_left, at.other_half()):
        signal(device)
    signal(at.across_y(y + 1))
    signal(at.across_y(y - 1))
    pl.semaphore_wait(pltpu.get_barrier_semaphore(), 19)

    unsent = []

    def send(src, dst, sems, index, device):
        copy = push(src, dst, sems, index, device)
        unsent.append(copy)
        return copy

    def move(src, dst, index):
        copy = pltpu.make_async_copy(src, dst, local_sem.at[index])
        copy.start()
        return copy

    def columns_of(half, to):
        return pl.ds(pl.multiple_of((half * 4 + to) * 512, 512), 512)

    halves = [
        (rows.at[:, columns_of(half, x)], pl.ds(half * 512, 512)) for half in (0, 1)
    ]
    z_rights, z_lefts = [], []
    for half, (origin, lanes) in enumerate(halves):
        z_rights.append(send(origin, rows_z.at[1, :, lanes], z_sem, half, z_right))
        z_lefts.append(send(origin, rows_z.at[2, :, lanes], z_sem, 2 + half, z_left))
    moved_rows = [
        move(origin, rows_z.at[0, :, lanes], half * 11 + 1)
        for half, (origin, lanes) in enumerate(halves)
    ]

    here = message_z.at[:, z_lo // 4, z_lo % 4]
    moved_z = move(message.at[:, z_lo // 4, z_lo % 4], here, 0)
    by_z = [
        send(message.at[:, ((z_lo + step) % 8) // 4, (z_lo + step) % 4], here,
             message_sem, step, same_half(step))
        for step in range(1, 8)
    ]

    weights = ((up, up_all), (down, down_all))

    def first_weight(w):
        return [
            send(weights[w][0].at[:, columns_of(way, (x + 2) % 4)], relay.at[w, way],
                 relay_sem, w * 2 + way, device)
            for way, device in ((0, x_right), (1, x_left))
        ]

    def direct_weight(w):
        origin, dst = weights[w]
        direct = []
        for way, device, to in ((0, x_right, (x + 1) % 4), (1, x_left, (x + 3) % 4)):
            for half in (0, 1):
                direct.append(
                    send(origin.at[:, columns_of(half, to)], dst.at[half, x],
                         weight_sem, w * 4 + way * 2 + half, device)
                )
        for half in (0, 1):
            direct.append(move(origin.at[:, columns_of(half, x)], dst.at[half, x], 2 + w * 2 + half))
        return direct

    def pass_weight(w, first, direct):
        dst = weights[w][1]
        for way, device, source in ((0, x_right, (x + 3) % 4), (1, x_left, (x + 1) % 4)):
            first[way].wait_recv()
            direct.append(
                send(relay.at[w, way], dst.at[way, source], relay_sem, 4 + w * 2 + way, device)
            )

    def arrive(copies, own=()):
        for copy in copies:
            copy.wait_recv()
        for copy in own:
            copy.wait()

    up_first, up_direct = first_weight(0), direct_weight(0)

    blocks = [z_lo]
    for order in range(1, 8):
        step = (order + 1) // 2
        blocks.append((z_lo - step + 8) % 8 if order % 2 == 1 else (z_lo + step) % 8)

    def next_rows(order):
        if order == 1:
            arrive(z_rights[:2])
        elif order == 2:
            arrive(z_lefts[:2])
        elif order % 2 == 1:
            z_rights[order // 2 + 1].wait_recv()
        else:
            z_lefts[order // 2].wait_recv()
        here = rows_z.at[order]
        if order in (1, 3, 5):
            z_rights.append(send(here, rows_z.at[order + 2], z_sem, 3 + order, z_right))
        elif order in (2, 4):
            z_lefts.append(send(here, rows_z.at[order + 2], z_sem, 3 + order, z_left))

    right_y, left_y, far_y = (y + 1) % 4, (y + 3) % 4, (y + 2) % 4
    near_rows, twin_rows, rows_first, rows_onward, own_rows = [], [], [], [], []
    mine = y * 2 + core

    def send_rows(pair):
        value = jnp.dot(
            pick[pair],
            rows_z[pair * 2 : pair * 2 + 2].reshape(64, 1024),
            preferred_element_type=F32,
        )
        slots_out[pair] = value.astype(BF16).reshape(8, 16, 1024)
        here = picked.at[mine, pair]
        for way, device, rel in ((0, y_right, 0), (1, y_left, 1)):
            expert = far_y * 2 + (core if rel == 0 else 1 - core)
            rows_first.append(
                send(slots_out.at[pair, expert], rows_relay.at[way, pair],
                     rows_relay_sem, pair * 2 + way, device)
            )
        for way, to in ((0, right_y), (1, left_y)):
            for rel, device in ((0, at.at_y(to)), (1, at.across_y(to))):
                expert = to * 2 + (core if rel == 0 else 1 - core)
                near_rows.append(
                    send(slots_out.at[pair, expert], here, y_sem, pair * 4 + way * 2 + rel, device)
                )
        twin_rows.append(send(slots_out.at[pair, y * 2 + 1 - core], here, twin_sem, pair, twin))
        own_rows.append(move(slots_out.at[pair, mine], here, 13 + pair))

    def pass_rows(pair):
        for way, device, source in (
            (0, at.at_y(right_y), left_y), (1, at.across_y(left_y), right_y)
        ):
            rows_first[pair * 2 + way].wait_recv()
            rows_onward.append(
                send(rows_relay.at[way, pair], picked.at[source * 2 + core, pair],
                     rows_relay_sem, 8 + pair * 2 + way, device)
            )

    def spread_rows(messages, first, count):
        tile = one_hot(iota((128, count), 0) == first + iota((128, count), 1) % 32)
        return jnp.dot(messages, tile, preferred_element_type=F32).astype(BF16)

    next_rows(1)
    next_rows(2)
    arrive(by_z, [moved_z])
    moved_y = move(message_z.at[:, :, :, y], message_y.at[:, :, :, y], 6)
    by_y = [
        send(message_z.at[:, :, :, (y + step) % 4], message_y.at[:, :, :, y],
             message_sem, 7 + step, at.at_y(y + step))
        for step in (1, 2, 3)
    ]

    passed = jnp.concatenate(
        [message_z[0, block // 4, block % 4].reshape(8, 128) for block in blocks], axis=0
    ).astype(BF16)
    slots, source = iota((512, 64), 0), iota((512, 64), 1)
    expand = one_hot(
        source == ((slots // 128) * 2 + (slots // 8) % 2) * 8 + (slots // 16) % 8
    )
    code = jnp.dot(expand, spread_rows(passed, 64, 64), preferred_element_type=F32)
    match = (
        (code == (slots % 2 + 1).astype(F32))
        & (source // 32 == (slots // 8) % 2)
        & ((source // 8) % 4 == (slots // 2) % 4)
    )
    pick[...] = one_hot(match).reshape(4, 128, 64)

    arrive(by_y, [moved_y])
    here = message_own.at[:, :, :, :, core]
    moved_core = move(message_y.at[:, :, :, :, core], here, 7)
    by_core = send(message_y.at[:, :, :, :, 1 - core], here, message_sem, 0, twin)
    next_rows(3)
    arrive([], moved_rows)
    send_rows(0)
    arrive([by_core], [moved_core])
    right_rows[...] = message_own[1].reshape(64, 128)
    entries[tensor] = jnp.concatenate(
        [right_rows[pl.ds(b, 16, stride=4), :] for b in range(4)], axis=1
    ).astype(BF16)
    here = entries.at[tensor]
    across = send(here, here, spread_sem, 0, at.other_half())
    spread = [send(here, here, spread_sem, step, at.at_x(x + step)) for step in (1, 2, 3)]
    moved_left = move(message_own.at[0, :, x], left_in_x.at[x], 17)
    spread += [
        send(message_own.at[0, :, (x + step) % 4], left_in_x.at[x],
             spread_sem, 6 + step, at.at_x(x + step))
        for step in (1, 2, 3)
    ]
    next_rows(4)
    send_rows(1)
    next_rows(5)
    pass_weight(0, up_first, up_direct)
    down_first = first_weight(1)
    send_rows(2)
    pass_rows(0)
    next_rows(6)
    next_rows(7)
    send_rows(3)
    pass_rows(1)
    across.wait_recv()
    here = entries.at[(1 - at.z_hi) * 4 + x]
    spread += [send(here, here, spread_sem, 3 + step, at.at_x(x + step)) for step in (1, 2, 3)]
    down_direct = direct_weight(1)
    pass_rows(2)
    pass_rows(3)

    codes, gates = spread_rows(passed, 64, 256), spread_rows(passed, 96, 256)

    @pl.loop(0, 8)
    def _(expert):
        slots, source = iota((64, 64), 0), iota((64, 64), 1)
        expand = one_hot(source == (slots // 8) * 8 + expert)
        code = jnp.dot(expand, codes, preferred_element_type=F32)
        gate = jnp.dot(expand, gates, preferred_element_type=F32)
        slots, places = iota((64, 256), 0), iota((64, 256), 1)
        match = (
            (code == (slots % 2 + 1).astype(F32))
            & (places // 32 == slots // 8)
            & ((places // 8) % 4 == (slots // 2) % 4)
        )
        value = jnp.where(match, gate, 0.0).astype(BF16)
        for part_at in (0, 1):
            combine[part_at, expert] = value[
                part_at * 32 : part_at * 32 + 32, part_at * 128 : part_at * 128 + 128
            ]

    for rr in range(2):
        for c in range(3):
            for b in range(4):
                k, n = iota((128, 128), 0), iota((128, 128), 1)
                here = (k // 2 + b * 48 == c * 64 + n % 64) & (k % 2 == rr) & (k < 96)
                order_map[b * 128 : b * 128 + 128, (rr * 3 + c) * 128 : (rr * 3 + c) * 128 + 128] = (
                    one_hot(here)
                )
    arrive(spread, [moved_left])

    placed = jnp.dot(
        entries[...].reshape(128, 512), order_map[...], preferred_element_type=F32
    )
    for t in range(8):
        for rr in range(2):
            for c in range(3):
                lanes = slice((rr * 3 + c) * 128, (rr * 3 + c) * 128 + 128)
                right_all[t * 2 + rr, pl.ds(c, 16, stride=3), :] = (
                    placed[t * 16 : t * 16 + 16, lanes]
                )

    arrive(up_direct[:4] + up_direct[6:], up_direct[4:6])

    widen = jnp.where(iota((8, 512), 1) // 64 == iota((8, 512), 0), 1.0, 0.0)

    def weigh(group):
        @pl.loop(0, 2)
        def _(half):
            left = left_in_x[group, half].reshape(8, 128)
            left_all[...] = contract_first(left, widen)
            for j in range(4):
                for lane in range(4):
                    lanes = slice(lane * 128, lane * 128 + 128)
                    delta = jnp.zeros((48, 128), F32)
                    for r in range(16):
                        delta = delta + right_all[r] * left_all[r * 4 + j : r * 4 + j + 1, lanes]
                    units = slice(j * 48, j * 48 + 48)
                    weight[group, half, units, lanes] = (
                        up_all[half, group, units, lanes].astype(F32) + delta
                    ).astype(BF16)

    def project(group, ab):
        total = jnp.zeros((192, 256), F32)
        for half in (0, 1):
            here = picked[:, ab * 2 : ab * 2 + 2, :, half * 512 : half * 512 + 512]
            total = total + lax.dot_general(
                weight[group, half], here.reshape(256, 512),
                (((1,), (1,)), ((), ())), preferred_element_type=F32,
            )
        part[ab, group] = total.astype(BF16)

    both = (0, 1)
    right_x, left_x, far_x = (x + 1) % 4, (x + 3) % 4, (x + 2) % 4
    top, low = pl.ds(0, 96), pl.ds(96, 96)
    far_parts, near_parts = [], [[], []]
    weigh(far_x)
    for ab in both:
        arrive(
            near_rows[ab * 8 : ab * 8 + 8] + twin_rows[ab * 2 : ab * 2 + 2]
            + rows_onward[ab * 4 : ab * 4 + 4],
            own_rows[ab * 2 : ab * 2 + 2],
        )
        project(far_x, ab)
        far_parts.append([
            send(part.at[ab, far_x, top], hidden_far.at[ab, 0], hidden_sem, ab * 6, x_right),
            send(part.at[ab, far_x, low], hidden_far.at[ab, 1], hidden_sem, ab * 6 + 1, x_left),
        ])
    weigh(right_x)
    for ab in both:
        project(right_x, ab)
        near_parts[ab].append(
            send(part.at[ab, right_x, low], hidden_near.at[ab, 0, low], hidden_sem, ab * 6 + 2, x_right)
        )
    weigh(left_x)
    for ab in both:
        project(left_x, ab)
        near_parts[ab].append(
            send(part.at[ab, left_x, top], hidden_near.at[ab, 1, top], hidden_sem, ab * 6 + 3, x_left)
        )
    for ab in both:
        for way, device, to, units in ((0, x_right, right_x, top), (1, x_left, left_x, low)):
            far_parts[ab][way].wait_recv()
            hidden_pass[ab, way] = (
                part[ab, to, units].astype(F32) + hidden_far[ab, way].astype(F32)
            ).astype(BF16)
            near_parts[ab].append(
                send(hidden_pass.at[ab, way], hidden_near.at[ab, way, units],
                     hidden_sem, ab * 6 + 4 + way, device)
            )
    pass_weight(1, down_first, down_direct)
    weigh(x)
    for ab in both:
        project(x, ab)
    gathers = []
    for ab in both:
        arrive(near_parts[ab])
        value = (
            part[ab, x].astype(F32)
            + hidden_near[ab, 0].astype(F32) + hidden_near[ab, 1].astype(F32)
        )
        hidden[ab, x] = (value / (1.0 + jnp.exp(-value))).astype(BF16)
        here = hidden.at[ab, x]
        gathers.append([
            send(here, here, gather_sem, ab * 4, x_right),
            send(here, here, gather_sem, ab * 4 + 1, x_left),
        ])
    for ab in both:
        for way, device, source, units in ((0, x_right, left_x, top), (1, x_left, right_x, low)):
            gathers[ab][way].wait_recv()
            here = hidden.at[ab, source, units]
            gathers[ab].append(send(here, here, gather_sem, ab * 4 + 2 + way, device))
    arrive(down_direct[:4] + down_direct[6:], down_direct[4:6])

    twins, relayed, direct, onward = [], [[], []], [[], []], [[], []]
    own_slots = [[], []]
    for ab in both:
        arrive(gathers[ab][2:])
        for half in (0, 1):
            value = contract_first(
                hidden[ab].reshape(768, 256), down_all[half].reshape(768, 512)
            )
            result[ab, :, :, :, half * 512 : half * 512 + 512] = (
                value.astype(BF16).reshape(4, 2, 32, 512)
            )
        twins.append(send(result.at[ab, :, 1 - core], twin_in.at[ab], core_sem, ab, twin))
        relayed[ab].append(
            send(result.at[ab, far_y, core], slots_relay.at[ab, 0], slots_relay_sem, ab, y_right)
        )
        here = slots_in.at[ab, y, core]
        direct[ab].append(send(result.at[ab, right_y, core], here, slots_sem, ab * 2, y_right))
        direct[ab].append(send(result.at[ab, left_y, core], here, slots_sem, ab * 2 + 1, y_left))
        own_slots[ab].append(move(result.at[ab, y, core], here, 8 + ab))

    def pass_twin(ab):
        twins[ab].wait_recv()
        relayed[ab].append(
            send(twin_in.at[ab, far_y], slots_relay.at[ab, 1], slots_relay_sem, 2 + ab, y_left)
        )
        here = slots_in.at[ab, y, 1 - core]
        direct[ab].append(send(twin_in.at[ab, right_y], here, slots_sem, 4 + ab * 2, y_right))
        direct[ab].append(send(twin_in.at[ab, left_y], here, slots_sem, 5 + ab * 2, y_left))
        own_slots[ab].append(move(twin_in.at[ab, y], here, 10 + ab))

    def pass_slots(ab, way):
        device, source, from_core = ((y_right, left_y, core), (y_left, right_y, 1 - core))[way]
        relayed[ab][way].wait_recv()
        onward[ab].append(
            send(slots_relay.at[ab, way], slots_in.at[ab, source, from_core],
                 slots_relay_sem, 4 + way * 2 + ab, device)
        )

    def mix_slots(ab):
        arrive(direct[ab] + onward[ab], own_slots[ab])
        value = contract_first(
            combine[ab].reshape(256, 128), slots_in[ab].reshape(256, 1024)
        )
        for order in range(4):
            for half in (0, 1):
                line[half * 8 + blocks[ab * 4 + order]] = (
                    value[order * 32 : order * 32 + 32, half * 512 : half * 512 + 512]
                )

    pass_twin(0)
    pass_slots(0, 0)
    pass_twin(1)
    pass_slots(0, 1)
    pass_slots(1, 0)
    mix_slots(0)
    pass_slots(1, 1)
    mix_slots(1)

    rights, lefts = [], []
    pieces = (slice(0, 16), slice(16, 32))
    for step in range(8):
        for piece, rows_at in enumerate(pieces):
            value = line[(z + 8 - step) % 16, rows_at]
            if step > 0:
                rights[step * 2 - 2 + piece].wait_recv()
                value = value + right_in[step - 1, rows_at].astype(F32)
            right_out[step, rows_at] = value.astype(BF16)
            there = pl.ds(piece * 16, 16)
            rights.append(
                send(right_out.at[step, there], right_in.at[step, there],
                     right_sem, step * 2 + piece, z_right)
            )
            if step < 7:
                value = line[(z + 9 + step) % 16, rows_at]
                if step > 0:
                    lefts[step * 2 - 2 + piece].wait_recv()
                    value = value + left_in[step - 1, rows_at].astype(F32)
                left_out[step, rows_at] = value.astype(BF16)
                lefts.append(
                    send(left_out.at[step, there], left_in.at[step, there],
                         left_sem, step * 2 + piece, z_left)
                )
    for piece, rows_at in enumerate(pieces):
        lefts[12 + piece].wait_recv()
        rights[14 + piece].wait_recv()
        value = line[z, rows_at] + right_in[7, rows_at].astype(F32) + left_in[6, rows_at].astype(F32)
        out[rows_at, :] = value.astype(BF16)
    for copy in unsent:
        copy.wait_send()


def layer(up, down, rows, message):
    any_space = pl.BlockSpec(memory_space=pl.ANY)
    return pl.pallas_call(
        layer_kernel,
        out_shape=jax.ShapeDtypeStruct((32, 512), BF16),
        in_specs=[any_space] * 4,
        out_specs=pl.BlockSpec(memory_space=pltpu.VMEM),
        scratch_shapes=[
            pltpu.VMEM((2, 4, 192, 512), BF16),
            pltpu.VMEM((2, 4, 192, 512), BF16),
            pltpu.VMEM((2, 2, 192, 512), BF16),
            pltpu.VMEM((8, 32, 1024), BF16),
            pltpu.VMEM((4, 8, 16, 1024), BF16),
            pltpu.VMEM((2, 4, 16, 1024), BF16),
            pltpu.VMEM((2, 2, 4, 4, 2, 1, 128), F32),
            pltpu.VMEM((2, 2, 4, 4, 2, 1, 128), F32),
            pltpu.VMEM((2, 2, 4, 4, 2, 1, 128), F32),
            pltpu.VMEM((4, 2, 4, 2, 1, 128), F32),
            pltpu.VMEM((4, 128, 64), BF16),
            pltpu.VMEM((2, 8, 32, 128), BF16),
            pltpu.VMEM((512, 768), BF16),
            pltpu.VMEM((64, 128), F32),
            pltpu.VMEM((8, 16, 512), BF16),
            pltpu.VMEM((16, 48, 128), F32),
            pltpu.VMEM((128, 512), F32),
            pltpu.VMEM((4, 2, 192, 512), BF16),
            pltpu.VMEM((8, 4, 16, 1024), BF16),
            pltpu.VMEM((2, 4, 192, 256), BF16),
            pltpu.VMEM((2, 2, 96, 256), BF16),
            pltpu.VMEM((2, 2, 192, 256), BF16),
            pltpu.VMEM((2, 2, 96, 256), BF16),
            pltpu.VMEM((2, 4, 192, 256), BF16),
            pltpu.VMEM((2, 4, 2, 32, 1024), BF16),
            pltpu.VMEM((2, 4, 32, 1024), BF16),
            pltpu.VMEM((2, 4, 2, 32, 1024), BF16),
            pltpu.VMEM((2, 2, 32, 1024), BF16),
            pltpu.VMEM((16, 32, 512), F32),
            pltpu.VMEM((8, 32, 512), BF16),
            pltpu.VMEM((7, 32, 512), BF16),
            pltpu.VMEM((8, 32, 512), BF16),
            pltpu.VMEM((7, 32, 512), BF16),
            pltpu.SemaphoreType.DMA((18,)),
            dma_sems(9),
            dma_sems(16),
            dma_sems(16),
            dma_sems(4),
            dma_sems(8),
            dma_sems(8),
            dma_sems(11),
            dma_sems(10),
            dma_sems(12),
            dma_sems(8),
            dma_sems(2),
            dma_sems(8),
            dma_sems(8),
            dma_sems(16),
            dma_sems(14),
        ],
        compiler_params=pltpu.CompilerParams(
            collective_id=0, has_side_effects=True, vmem_limit_bytes=VMEM_LIMIT
        ),
        name="layer",
    )(up, down, rows, message)


def body(
    core_left,
    core_right,
    grad_left,
    grad_right,
    first_left,
    first_right,
    second_left,
    second_right,
    up_base,
    down_base,
    states,
    routes,
    gates,
):
    cores = (
        core_left, core_right, grad_left, grad_right,
        first_left, first_right, second_left, second_right,
    )
    (
        left_next, right_next, first_left_next, first_right_next,
        second_left_next, second_right_next, message,
    ) = prepare(cores, routes.reshape(32, 8), gates.reshape(32, 8))
    mixed = layer(
        up_base[0], down_base[0], states.reshape(32, 4096), message.reshape(2, 2, 4, 4, 2, 1, 128)
    )
    mixed = mixed.reshape(4, 8, 512)
    return (
        mixed,
        left_next,
        right_next,
        first_left_next,
        first_right_next,
        second_left_next,
        second_right_next,
    )


def solution(mesh):
    cores = (P("tensor", "train"),) * 6
    in_specs = cores + (P("tensor", "train"),) * 2 + (
        P("train", "tensor", None),
        P("train", "tensor", None),
        P(None, "train", None),
        P(None, "train", None),
        P(None, "train", None),
    )
    out_specs = (P(None, "train", "tensor"),) + cores
    return jax.shard_map(body, mesh=mesh, in_specs=in_specs, out_specs=out_specs, check_vma=False)
```

```python
import jax
import jax.numpy as jnp
from jax import lax
from jax.experimental import pallas as pl
from jax.experimental.pallas import tpu as pltpu
from jax.sharding import PartitionSpec as P

MESH = pl.DeviceIdType.MESH
BF16 = jnp.bfloat16
F32 = jnp.float32

BETA_ONE = 0.9
BETA_TWO = 0.999
LEARN_RATE = 0.01
WEIGHT_DECAY = 0.1
EPSILON = 1e-08
STEP_NUMBER = 10.0

VMEM_LIMIT = 60 * 1024 * 1024


def adamw_update(value_now, gradient, first_moment, second_moment):
    first_next = BETA_ONE * first_moment + (1.0 - BETA_ONE) * gradient
    second_next = BETA_TWO * second_moment + (1.0 - BETA_TWO) * gradient * gradient
    first_scale = 1.0 - BETA_ONE**STEP_NUMBER
    second_scale = 1.0 - BETA_TWO**STEP_NUMBER
    update = first_next / first_scale / (jnp.sqrt(second_next / second_scale) + EPSILON)
    value_next = value_now - LEARN_RATE * (update + WEIGHT_DECAY * value_now)
    return (value_next, first_next, second_next)


def prepare_kernel(
    core_left, core_right, grad_left, grad_right, first_left, first_right, second_left, second_right,
    routes, gates,
    left_next, right_next, first_left_next, first_right_next, second_left_next, second_right_next,
    message, entries,
):
    left, first, second = adamw_update(
        core_left[...], grad_left[...], first_left[...], second_left[...]
    )
    left_next[...], first_left_next[...], second_left_next[...] = left, first, second
    right, first, second = adamw_update(
        core_right[...], grad_right[...], first_right[...], second_right[...]
    )
    right_next[...], first_right_next[...], second_right_next[...] = right, first, second

    for r in range(16):
        entries[0, r * 4 : r * 4 + 4] = left[:, r * 64 : r * 64 + 64]
    for pair in range(48):
        entries[1, pair * 2 : pair * 2 + 2] = right[:, pair * 64 : pair * 64 + 64]
    entries[1, 96:128] = jnp.zeros((32, 64), F32)
    expert = lax.broadcasted_iota(jnp.int32, (32, 64), 1)
    taken, weight = jnp.zeros((32, 64), F32), jnp.zeros((32, 64), F32)
    for k in range(8):
        chosen = routes[:, k : k + 1] == expert
        taken = taken + jnp.where(chosen, 1.0, 0.0)
        weight = weight + jnp.where(chosen, gates[:, k : k + 1], 0.0)
    to, by = (lax.broadcasted_iota(jnp.int32, (32, 32), dim) for dim in (0, 1))
    before = jnp.where((by < to) & (by // 8 == to // 8), 1.0, 0.0)
    earlier = jnp.dot(before, taken, preferred_element_type=F32)
    entries[0, 64:96] = taken * (earlier + 1.0)
    entries[0, 96:128] = weight
    row, column = (lax.broadcasted_iota(jnp.int32, (128, 128), dim) for dim in (0, 1))
    same = jnp.where(row == column, 1.0, 0.0).astype(BF16)
    for kind in range(2):
        message[kind] = lax.dot_general(
            entries[kind].astype(BF16), same, (((0,), (0,)), ((), ())), preferred_element_type=F32
        )


def prepare(cores, routes, gates):
    return pl.pallas_call(
        prepare_kernel,
        out_shape=(
            *(jax.ShapeDtypeStruct(shape, F32) for shape in ((4, 1024), (2, 3072)) * 3),
            jax.ShapeDtypeStruct((2, 64, 128), F32),
        ),
        scratch_shapes=[pltpu.VMEM((2, 128, 64), F32)],
        name="prepare",
    )(*cores, routes, gates)


class Place:
    def __init__(self):
        self.train = lax.axis_index("train")
        self.tensor = lax.axis_index("tensor")
        self.core = self.train % 2
        self.y = (self.train // 2) % 4
        self.z_lo = self.train // 8
        self.x = self.tensor % 4
        self.z_hi = self.tensor // 4
        self.z = self.z_hi * 8 + self.z_lo

    def at_z(self, z):
        z = (z + 16) % 16
        return ((z % 8) * 8 + self.y * 2 + self.core, (z // 8) * 4 + self.x)

    def at_y(self, y):
        return (self.z_lo * 8 + ((y + 4) % 4) * 2 + self.core, self.tensor)

    def at_x(self, x):
        return (self.train, self.z_hi * 4 + (x + 4) % 4)

    def across_y(self, y):
        return (self.z_lo * 8 + ((y + 4) % 4) * 2 + 1 - self.core, self.tensor)

    def twin(self):
        return (self.train + 1 - 2 * self.core, self.tensor)

    def other_half(self):
        return (self.train, (1 - self.z_hi) * 4 + self.x)


def push(src, dst, sems, index, device):
    copy = pltpu.make_async_remote_copy(
        src_ref=src,
        dst_ref=dst,
        send_sem=sems.at[0, index],
        recv_sem=sems.at[1, index],
        device_id=device,
        device_id_type=MESH,
    )
    copy.start()
    return copy


def signal(device):
    pl.semaphore_signal(
        pltpu.get_barrier_semaphore(), inc=1, device_id=device, device_id_type=MESH
    )


def dma_sems(count):
    return pltpu.SemaphoreType.DMA((2, count))


def iota(shape, dim):
    return lax.broadcasted_iota(jnp.int32, shape, dim)


def one_hot(condition):
    return jnp.where(condition, 1.0, 0.0).astype(BF16)


def contract_first(left, right):
    return lax.dot_general(left, right, (((0,), (0,)), ((), ())), preferred_element_type=F32)


def layer_kernel(
    up, down, rows, message, out,
    up_all, down_all, relay, rows_z, slots_out, rows_relay, message_z, message_y, message_own, left_in_x,
    pick, combine, order_map, right_rows, entries, right_all, left_all, weight, picked,
    part, hidden_far, hidden_near, hidden_pass, hidden,
    result, twin_in, slots_in, slots_relay, line, right_in, left_in, right_out, left_out,
    local_sem, z_sem, y_sem, rows_relay_sem, twin_sem, weight_sem, relay_sem,
    message_sem, spread_sem, hidden_sem, gather_sem,
    core_sem, slots_sem, slots_relay_sem, right_sem, left_sem,
):
    at = Place()
    tensor, x, y, z_lo, z, core = at.tensor, at.x, at.y, at.z_lo, at.z, at.core
    twin = at.twin()
    x_right, x_left = at.at_x(x + 1), at.at_x(x - 1)
    y_right, y_left = at.at_y(y + 1), at.at_y(y - 1)
    z_right, z_left = at.at_z(z + 1), at.at_z(z - 1)

    def same_half(step):
        return (((z_lo + step) % 8) * 8 + y * 2 + core, tensor)

    for step in range(1, 8):
        signal(same_half(step))
    for step in (1, 2, 3):
        signal(at.at_x(x + step))
        signal(at.at_y(y + step))
    for device in (twin, z_right, z_left, at.other_half()):
        signal(device)
    signal(at.across_y(y + 1))
    signal(at.across_y(y - 1))
    pl.semaphore_wait(pltpu.get_barrier_semaphore(), 19)

    unsent = []

    def send(src, dst, sems, index, device):
        copy = push(src, dst, sems, index, device)
        unsent.append(copy)
        return copy

    def move(src, dst, index):
        copy = pltpu.make_async_copy(src, dst, local_sem.at[index])
        copy.start()
        return copy

    def columns_of(half, to):
        return pl.ds(pl.multiple_of((half * 4 + to) * 512, 512), 512)

    halves = [
        (rows.at[:, columns_of(half, x)], pl.ds(half * 512, 512)) for half in (0, 1)
    ]
    z_rights, z_lefts = [], []
    for half, (origin, lanes) in enumerate(halves):
        z_rights.append(send(origin, rows_z.at[1, :, lanes], z_sem, half, z_right))
        z_lefts.append(send(origin, rows_z.at[2, :, lanes], z_sem, 2 + half, z_left))
    moved_rows = [
        move(origin, rows_z.at[0, :, lanes], half * 11 + 1)
        for half, (origin, lanes) in enumerate(halves)
    ]

    here = message_z.at[:, z_lo // 4, z_lo % 4]
    moved_z = move(message.at[:, z_lo // 4, z_lo % 4], here, 0)
    by_z = [
        send(message.at[:, ((z_lo + step) % 8) // 4, (z_lo + step) % 4], here,
             message_sem, step, same_half(step))
        for step in range(1, 8)
    ]

    weights = ((up, up_all), (down, down_all))

    def first_weight(w):
        return [
            send(weights[w][0].at[:, columns_of(way, (x + 2) % 4)], relay.at[w, way],
                 relay_sem, w * 2 + way, device)
            for way, device in ((0, x_right), (1, x_left))
        ]

    def direct_weight(w):
        origin, dst = weights[w]
        direct = []
        for way, device, to in ((0, x_right, (x + 1) % 4), (1, x_left, (x + 3) % 4)):
            for half in (0, 1):
                direct.append(
                    send(origin.at[:, columns_of(half, to)], dst.at[half, x],
                         weight_sem, w * 4 + way * 2 + half, device)
                )
        for half in (0, 1):
            direct.append(move(origin.at[:, columns_of(half, x)], dst.at[half, x], 2 + w * 2 + half))
        return direct

    def pass_weight(w, first, direct):
        dst = weights[w][1]
        for way, device, source in ((0, x_right, (x + 3) % 4), (1, x_left, (x + 1) % 4)):
            first[way].wait_recv()
            direct.append(
                send(relay.at[w, way], dst.at[way, source], relay_sem, 4 + w * 2 + way, device)
            )

    def arrive(copies, own=()):
        for copy in copies:
            copy.wait_recv()
        for copy in own:
            copy.wait()

    up_first, up_direct = first_weight(0), direct_weight(0)

    blocks = [z_lo]
    for order in range(1, 8):
        step = (order + 1) // 2
        blocks.append((z_lo - step + 8) % 8 if order % 2 == 1 else (z_lo + step) % 8)

    def next_rows(order):
        if order == 1:
            arrive(z_rights[:2])
        elif order == 2:
            arrive(z_lefts[:2])
        elif order % 2 == 1:
            z_rights[order // 2 + 1].wait_recv()
        else:
            z_lefts[order // 2].wait_recv()
        here = rows_z.at[order]
        if order in (1, 3, 5):
            z_rights.append(send(here, rows_z.at[order + 2], z_sem, 3 + order, z_right))
        elif order in (2, 4):
            z_lefts.append(send(here, rows_z.at[order + 2], z_sem, 3 + order, z_left))

    right_y, left_y, far_y = (y + 1) % 4, (y + 3) % 4, (y + 2) % 4
    near_rows, twin_rows, rows_first, rows_onward, own_rows = [], [], [], [], []
    mine = y * 2 + core

    def send_rows(pair):
        value = jnp.dot(
            pick[pair],
            rows_z[pair * 2 : pair * 2 + 2].reshape(64, 1024),
            preferred_element_type=F32,
        )
        slots_out[pair] = value.astype(BF16).reshape(8, 16, 1024)
        here = picked.at[mine, pair]
        for way, device, rel in ((0, y_right, 0), (1, y_left, 1)):
            expert = far_y * 2 + (core if rel == 0 else 1 - core)
            rows_first.append(
                send(slots_out.at[pair, expert], rows_relay.at[way, pair],
                     rows_relay_sem, pair * 2 + way, device)
            )
        for way, to in ((0, right_y), (1, left_y)):
            for rel, device in ((0, at.at_y(to)), (1, at.across_y(to))):
                expert = to * 2 + (core if rel == 0 else 1 - core)
                near_rows.append(
                    send(slots_out.at[pair, expert], here, y_sem, pair * 4 + way * 2 + rel, device)
                )
        twin_rows.append(send(slots_out.at[pair, y * 2 + 1 - core], here, twin_sem, pair, twin))
        own_rows.append(move(slots_out.at[pair, mine], here, 13 + pair))

    def pass_rows(pair):
        for way, device, source in (
            (0, at.at_y(right_y), left_y), (1, at.across_y(left_y), right_y)
        ):
            rows_first[pair * 2 + way].wait_recv()
            rows_onward.append(
                send(rows_relay.at[way, pair], picked.at[source * 2 + core, pair],
                     rows_relay_sem, 8 + pair * 2 + way, device)
            )

    def spread_rows(messages, first, count):
        tile = one_hot(iota((128, count), 0) == first + iota((128, count), 1) % 32)
        return jnp.dot(messages, tile, preferred_element_type=F32).astype(BF16)

    for rr in range(2):
        for c in range(3):
            for b in range(4):
                k, n = iota((128, 128), 0), iota((128, 128), 1)
                here = (k // 2 + b * 48 == c * 64 + n % 64) & (k % 2 == rr) & (k < 96)
                order_map[b * 128 : b * 128 + 128, (rr * 3 + c) * 128 : (rr * 3 + c) * 128 + 128] = (
                    one_hot(here)
                )

    next_rows(1)
    next_rows(2)
    arrive(by_z, [moved_z])
    moved_y = move(message_z.at[:, :, :, y], message_y.at[:, :, :, y], 6)
    by_y = [
        send(message_z.at[:, :, :, (y + step) % 4], message_y.at[:, :, :, y],
             message_sem, 7 + step, at.at_y(y + step))
        for step in (1, 2, 3)
    ]

    passed = jnp.concatenate(
        [message_z[0, block // 4, block % 4].reshape(8, 128) for block in blocks], axis=0
    ).astype(BF16)
    slots, source = iota((512, 64), 0), iota((512, 64), 1)
    expand = one_hot(
        source == ((slots // 128) * 2 + (slots // 8) % 2) * 8 + (slots // 16) % 8
    )
    code = jnp.dot(expand, spread_rows(passed, 64, 64), preferred_element_type=F32)
    match = (
        (code == (slots % 2 + 1).astype(F32))
        & (source // 32 == (slots // 8) % 2)
        & ((source // 8) % 4 == (slots // 2) % 4)
    )
    pick[...] = one_hot(match).reshape(4, 128, 64)

    arrive(by_y, [moved_y])
    here = message_own.at[:, :, :, :, core]
    moved_core = move(message_y.at[:, :, :, :, core], here, 7)
    by_core = send(message_y.at[:, :, :, :, 1 - core], here, message_sem, 0, twin)
    next_rows(3)
    arrive([], moved_rows)
    send_rows(0)
    arrive([by_core], [moved_core])
    right_rows[...] = message_own[1].reshape(64, 128)
    entries[tensor] = jnp.concatenate(
        [right_rows[pl.ds(b, 16, stride=4), :] for b in range(4)], axis=1
    ).astype(BF16)
    here = entries.at[tensor]
    across = send(here, here, spread_sem, 0, at.other_half())
    spread = [send(here, here, spread_sem, step, at.at_x(x + step)) for step in (1, 2, 3)]
    moved_left = move(message_own.at[0, :, x], left_in_x.at[x], 17)
    spread += [
        send(message_own.at[0, :, (x + step) % 4], left_in_x.at[x],
             spread_sem, 6 + step, at.at_x(x + step))
        for step in (1, 2, 3)
    ]
    next_rows(4)
    send_rows(1)
    next_rows(5)
    pass_weight(0, up_first, up_direct)
    down_first = first_weight(1)
    send_rows(2)
    pass_rows(0)
    next_rows(6)
    next_rows(7)
    send_rows(3)
    pass_rows(1)
    across.wait_recv()
    here = entries.at[(1 - at.z_hi) * 4 + x]
    spread += [send(here, here, spread_sem, 3 + step, at.at_x(x + step)) for step in (1, 2, 3)]
    down_direct = direct_weight(1)
    pass_rows(2)
    pass_rows(3)

    arrive(spread, [moved_left])

    placed = jnp.dot(
        entries[...].reshape(128, 512), order_map[...], preferred_element_type=F32
    )
    for t in range(8):
        for rr in range(2):
            for c in range(3):
                lanes = slice((rr * 3 + c) * 128, (rr * 3 + c) * 128 + 128)
                right_all[t * 2 + rr, pl.ds(c, 16, stride=3), :] = (
                    placed[t * 16 : t * 16 + 16, lanes]
                )

    arrive(up_direct[:4] + up_direct[6:], up_direct[4:6])

    widen = jnp.where(iota((8, 512), 1) // 64 == iota((8, 512), 0), 1.0, 0.0)

    def weigh(group):
        @pl.loop(0, 2)
        def _(half):
            left = left_in_x[group, half].reshape(8, 128)
            left_all[...] = contract_first(left, widen)
            for j in range(4):
                for lane in range(4):
                    lanes = slice(lane * 128, lane * 128 + 128)
                    delta = jnp.zeros((48, 128), F32)
                    for r in range(16):
                        delta = delta + right_all[r] * left_all[r * 4 + j : r * 4 + j + 1, lanes]
                    units = slice(j * 48, j * 48 + 48)
                    weight[group, half, units, lanes] = (
                        up_all[half, group, units, lanes].astype(F32) + delta
                    ).astype(BF16)

    def project(group, ab):
        total = jnp.zeros((192, 256), F32)
        for half in (0, 1):
            here = picked[:, ab * 2 : ab * 2 + 2, :, half * 512 : half * 512 + 512]
            total = total + lax.dot_general(
                weight[group, half], here.reshape(256, 512),
                (((1,), (1,)), ((), ())), preferred_element_type=F32,
            )
        part[ab, group] = total.astype(BF16)

    both = (0, 1)
    right_x, left_x, far_x = (x + 1) % 4, (x + 3) % 4, (x + 2) % 4
    top, low = pl.ds(0, 96), pl.ds(96, 96)
    far_parts, near_parts = [], [[], []]
    weigh(far_x)
    for ab in both:
        arrive(
            near_rows[ab * 8 : ab * 8 + 8] + twin_rows[ab * 2 : ab * 2 + 2]
            + rows_onward[ab * 4 : ab * 4 + 4],
            own_rows[ab * 2 : ab * 2 + 2],
        )
        project(far_x, ab)
        far_parts.append([
            send(part.at[ab, far_x, top], hidden_far.at[ab, 0], hidden_sem, ab * 6, x_right),
            send(part.at[ab, far_x, low], hidden_far.at[ab, 1], hidden_sem, ab * 6 + 1, x_left),
        ])
    weigh(right_x)
    for ab in both:
        project(right_x, ab)
        near_parts[ab].append(
            send(part.at[ab, right_x, low], hidden_near.at[ab, 0, low], hidden_sem, ab * 6 + 2, x_right)
        )
    weigh(left_x)
    for ab in both:
        project(left_x, ab)
        near_parts[ab].append(
            send(part.at[ab, left_x, top], hidden_near.at[ab, 1, top], hidden_sem, ab * 6 + 3, x_left)
        )
    for ab in both:
        for way, device, to, units in ((0, x_right, right_x, top), (1, x_left, left_x, low)):
            far_parts[ab][way].wait_recv()
            hidden_pass[ab, way] = (
                part[ab, to, units].astype(F32) + hidden_far[ab, way].astype(F32)
            ).astype(BF16)
            near_parts[ab].append(
                send(hidden_pass.at[ab, way], hidden_near.at[ab, way, units],
                     hidden_sem, ab * 6 + 4 + way, device)
            )
    pass_weight(1, down_first, down_direct)
    weigh(x)
    for ab in both:
        project(x, ab)
    gathers = []
    for ab in both:
        arrive(near_parts[ab])
        value = (
            part[ab, x].astype(F32)
            + hidden_near[ab, 0].astype(F32) + hidden_near[ab, 1].astype(F32)
        )
        hidden[ab, x] = (value / (1.0 + jnp.exp(-value))).astype(BF16)
        here = hidden.at[ab, x]
        gathers.append([
            send(here, here, gather_sem, ab * 4, x_right),
            send(here, here, gather_sem, ab * 4 + 1, x_left),
        ])
    for ab in both:
        for way, device, source, units in ((0, x_right, left_x, top), (1, x_left, right_x, low)):
            gathers[ab][way].wait_recv()
            here = hidden.at[ab, source, units]
            gathers[ab].append(send(here, here, gather_sem, ab * 4 + 2 + way, device))

    codes, gates = spread_rows(passed, 64, 256), spread_rows(passed, 96, 256)

    @pl.loop(0, 8)
    def _(expert):
        slots, source = iota((64, 64), 0), iota((64, 64), 1)
        expand = one_hot(source == (slots // 8) * 8 + expert)
        code = jnp.dot(expand, codes, preferred_element_type=F32)
        gate = jnp.dot(expand, gates, preferred_element_type=F32)
        slots, places = iota((64, 256), 0), iota((64, 256), 1)
        match = (
            (code == (slots % 2 + 1).astype(F32))
            & (places // 32 == slots // 8)
            & ((places // 8) % 4 == (slots // 2) % 4)
        )
        value = jnp.where(match, gate, 0.0).astype(BF16)
        for part_at in (0, 1):
            combine[part_at, expert] = value[
                part_at * 32 : part_at * 32 + 32, part_at * 128 : part_at * 128 + 128
            ]

    arrive(down_direct[:4] + down_direct[6:], down_direct[4:6])

    twins, relayed, direct, onward = [], [[], []], [[], []], [[], []]
    own_slots = [[], []]

    def pass_twin(ab):
        twins[ab].wait_recv()
        relayed[ab].append(
            send(twin_in.at[ab, far_y], slots_relay.at[ab, 1], slots_relay_sem, 2 + ab, y_left)
        )
        here = slots_in.at[ab, y, 1 - core]
        direct[ab].append(send(twin_in.at[ab, right_y], here, slots_sem, 4 + ab * 2, y_right))
        direct[ab].append(send(twin_in.at[ab, left_y], here, slots_sem, 5 + ab * 2, y_left))
        own_slots[ab].append(move(twin_in.at[ab, y], here, 10 + ab))

    for ab in both:
        arrive(gathers[ab][2:])
        if ab == 1:
            pass_twin(0)
        turned = hidden[ab].reshape(768, 256).T
        for half in (0, 1):
            value = jnp.dot(
                turned, down_all[half].reshape(768, 512), preferred_element_type=F32
            )
            result[ab, :, :, :, half * 512 : half * 512 + 512] = (
                value.astype(BF16).reshape(4, 2, 32, 512)
            )
        twins.append(send(result.at[ab, :, 1 - core], twin_in.at[ab], core_sem, ab, twin))
        relayed[ab].append(
            send(result.at[ab, far_y, core], slots_relay.at[ab, 0], slots_relay_sem, ab, y_right)
        )
        here = slots_in.at[ab, y, core]
        direct[ab].append(send(result.at[ab, right_y, core], here, slots_sem, ab * 2, y_right))
        direct[ab].append(send(result.at[ab, left_y, core], here, slots_sem, ab * 2 + 1, y_left))
        own_slots[ab].append(move(result.at[ab, y, core], here, 8 + ab))

    def pass_slots(ab, way):
        device, source, from_core = ((y_right, left_y, core), (y_left, right_y, 1 - core))[way]
        relayed[ab][way].wait_recv()
        onward[ab].append(
            send(slots_relay.at[ab, way], slots_in.at[ab, source, from_core],
                 slots_relay_sem, 4 + way * 2 + ab, device)
        )

    def mix_slots(ab):
        arrive(direct[ab] + onward[ab], own_slots[ab])
        value = contract_first(
            combine[ab].reshape(256, 128), slots_in[ab].reshape(256, 1024)
        )
        for order in range(4):
            for half in (0, 1):
                line[half * 8 + blocks[ab * 4 + order]] = (
                    value[order * 32 : order * 32 + 32, half * 512 : half * 512 + 512]
                )

    pass_slots(0, 0)
    pass_twin(1)
    pass_slots(0, 1)
    pass_slots(1, 0)
    mix_slots(0)
    pass_slots(1, 1)
    mix_slots(1)

    rights, lefts = [], []
    pieces = (slice(0, 16), slice(16, 32))
    for step in range(8):
        for piece, rows_at in enumerate(pieces):
            value = line[(z + 8 - step) % 16, rows_at]
            if step > 0:
                rights[step * 2 - 2 + piece].wait_recv()
                value = value + right_in[step - 1, rows_at].astype(F32)
            right_out[step, rows_at] = value.astype(BF16)
            there = pl.ds(piece * 16, 16)
            rights.append(
                send(right_out.at[step, there], right_in.at[step, there],
                     right_sem, step * 2 + piece, z_right)
            )
            if step < 7:
                value = line[(z + 9 + step) % 16, rows_at]
                if step > 0:
                    lefts[step * 2 - 2 + piece].wait_recv()
                    value = value + left_in[step - 1, rows_at].astype(F32)
                left_out[step, rows_at] = value.astype(BF16)
                lefts.append(
                    send(left_out.at[step, there], left_in.at[step, there],
                         left_sem, step * 2 + piece, z_left)
                )
    for piece, rows_at in enumerate(pieces):
        lefts[12 + piece].wait_recv()
        rights[14 + piece].wait_recv()
        value = line[z, rows_at] + right_in[7, rows_at].astype(F32) + left_in[6, rows_at].astype(F32)
        out[rows_at, :] = value.astype(BF16)
    for copy in unsent:
        copy.wait_send()


def layer(up, down, rows, message):
    any_space = pl.BlockSpec(memory_space=pl.ANY)
    return pl.pallas_call(
        layer_kernel,
        out_shape=jax.ShapeDtypeStruct((32, 512), BF16),
        in_specs=[any_space] * 4,
        out_specs=pl.BlockSpec(memory_space=pltpu.VMEM),
        scratch_shapes=[
            pltpu.VMEM((2, 4, 192, 512), BF16),
            pltpu.VMEM((2, 4, 192, 512), BF16),
            pltpu.VMEM((2, 2, 192, 512), BF16),
            pltpu.VMEM((8, 32, 1024), BF16),
            pltpu.VMEM((4, 8, 16, 1024), BF16),
            pltpu.VMEM((2, 4, 16, 1024), BF16),
            pltpu.VMEM((2, 2, 4, 4, 2, 1, 128), F32),
            pltpu.VMEM((2, 2, 4, 4, 2, 1, 128), F32),
            pltpu.VMEM((2, 2, 4, 4, 2, 1, 128), F32),
            pltpu.VMEM((4, 2, 4, 2, 1, 128), F32),
            pltpu.VMEM((4, 128, 64), BF16),
            pltpu.VMEM((2, 8, 32, 128), BF16),
            pltpu.VMEM((512, 768), BF16),
            pltpu.VMEM((64, 128), F32),
            pltpu.VMEM((8, 16, 512), BF16),
            pltpu.VMEM((16, 48, 128), F32),
            pltpu.VMEM((128, 512), F32),
            pltpu.VMEM((4, 2, 192, 512), BF16),
            pltpu.VMEM((8, 4, 16, 1024), BF16),
            pltpu.VMEM((2, 4, 192, 256), BF16),
            pltpu.VMEM((2, 2, 96, 256), BF16),
            pltpu.VMEM((2, 2, 192, 256), BF16),
            pltpu.VMEM((2, 2, 96, 256), BF16),
            pltpu.VMEM((2, 4, 192, 256), BF16),
            pltpu.VMEM((2, 4, 2, 32, 1024), BF16),
            pltpu.VMEM((2, 4, 32, 1024), BF16),
            pltpu.VMEM((2, 4, 2, 32, 1024), BF16),
            pltpu.VMEM((2, 2, 32, 1024), BF16),
            pltpu.VMEM((16, 32, 512), F32),
            pltpu.VMEM((8, 32, 512), BF16),
            pltpu.VMEM((7, 32, 512), BF16),
            pltpu.VMEM((8, 32, 512), BF16),
            pltpu.VMEM((7, 32, 512), BF16),
            pltpu.SemaphoreType.DMA((18,)),
            dma_sems(9),
            dma_sems(16),
            dma_sems(16),
            dma_sems(4),
            dma_sems(8),
            dma_sems(8),
            dma_sems(11),
            dma_sems(10),
            dma_sems(12),
            dma_sems(8),
            dma_sems(2),
            dma_sems(8),
            dma_sems(8),
            dma_sems(16),
            dma_sems(14),
        ],
        compiler_params=pltpu.CompilerParams(
            collective_id=0, has_side_effects=True, vmem_limit_bytes=VMEM_LIMIT
        ),
        name="layer",
    )(up, down, rows, message)


def body(
    core_left,
    core_right,
    grad_left,
    grad_right,
    first_left,
    first_right,
    second_left,
    second_right,
    up_base,
    down_base,
    states,
    routes,
    gates,
):
    cores = (
        core_left, core_right, grad_left, grad_right,
        first_left, first_right, second_left, second_right,
    )
    (
        left_next, right_next, first_left_next, first_right_next,
        second_left_next, second_right_next, message,
    ) = prepare(cores, routes.reshape(32, 8), gates.reshape(32, 8))
    mixed = layer(
        up_base[0], down_base[0], states.reshape(32, 4096), message.reshape(2, 2, 4, 4, 2, 1, 128)
    )
    mixed = mixed.reshape(4, 8, 512)
    return (
        mixed,
        left_next,
        right_next,
        first_left_next,
        first_right_next,
        second_left_next,
        second_right_next,
    )


def solution(mesh):
    cores = (P("tensor", "train"),) * 6
    in_specs = cores + (P("tensor", "train"),) * 2 + (
        P("train", "tensor", None),
        P("train", "tensor", None),
        P(None, "train", None),
        P(None, "train", None),
        P(None, "train", None),
    )
    out_specs = (P(None, "train", "tensor"),) + cores
    return jax.shard_map(body, mesh=mesh, in_specs=in_specs, out_specs=out_specs, check_vma=False)
```
